1024 devices in a mesh: dp: 64 (over y, x, z_hi), group: 16 (over z_lo, core).
Axes of the slice: x: 4, y: 8, z: 16 (z_hi: 2, z_lo: 8; z = z_hi * 8 + z_lo), core: 2. Of those that a mesh axis runs over, the one named last changes fastest.
Arguments:
- images: bfloat16 [12288, 1152], P(('dp', 'group')), may hold values from -0.29882812 to 0.29882812
- texts: bfloat16 [12288, 1152], P(('dp', 'group')), may hold values from -0.29882812 to 0.29882812
- log_scale: float32 [1], replicated, may hold values from 2.3 to 3.4
- bias: float32 [1], replicated, may hold values from -5 to -2
Outputs:
- image_grad: float32 [12288, 1152], P(('dp', 'group'))
- text_grad: float32 [12288, 1152], P(('dp', 'group'))
- statistics: float32 [2], replicated
The draws below stay inside these ranges and needn't reach their ends.
All inputs are finite; a program needn't handle non-finite values.
Results may differ from the reference program's by a relative error of at most 0.002.
The reference program's roundings to bfloat16 on the way (of `weight_b`) count: a program that leaves them out, or rounds other values in their place, can miss the bound.
Values may be sent and summed in bfloat16 or wider, within the bound.
A program may use at most 32 MiB of HBM per device.

```python
import math
import jax
import jax.numpy as jnp
from jax import lax

D = 1152
PAIRS = 12288


def shard_levels(stream_key, dims, split, smallest, high):
    factor_of = 1.0
    for position, parts in split:
        steps = jax.random.uniform(jax.random.fold_in(jax.random.fold_in(stream_key, 6), position), (parts,), jnp.float32, smallest / len(split), high / len(split))
        factor_of = factor_of * jnp.repeat(jnp.exp(steps), dims[position] // parts).reshape((-1,) + (1,) * (len(dims) - 1 - position))
    return factor_of


def bell_draw(own_key, dims, width, reach, pieces=(), held_as=jnp.bfloat16):
    drawn = width * jax.random.normal(own_key, dims, jnp.float32)
    if pieces:
        drawn = drawn * shard_levels(own_key, dims, pieces, -0.22, 0.18)
    return jnp.clip(drawn, -reach, reach).astype(held_as)


def setup_inputs(seed: int = 0) -> dict:
    arg_keys = jax.random.split(jax.random.key(seed), 5)
    images = bell_draw(arg_keys[0], (PAIRS, D), 0.05, 0.29882812, ((0, 1024),))
    texts = bell_draw(arg_keys[1], (PAIRS, D), 0.05, 0.29882812, ((0, 1024),))
    log_scale = jnp.clip(jax.random.uniform(arg_keys[2], (1,), jnp.float32, 2.3, 3.4), 2.3, 3.4)
    bias = jnp.clip(jax.random.uniform(arg_keys[3], (1,), jnp.float32, -5.0, -2.0), -5.0, -2.0)
    return {"images": images, "texts": texts, "log_scale": log_scale, "bias": bias}


def unit_rows(values):
    full = values.astype(jnp.float32)
    inverse = lax.rsqrt(lax.optimization_barrier(jnp.sum(full * full, axis=1, keepdims=True)) + 1e-06)
    return (full * inverse, inverse)

def reference(images, texts, log_scale, bias):
    img_unit, inv_img = unit_rows(images)
    txt_unit, inv_txt = unit_rows(texts)
    img_b = img_unit.astype(jnp.bfloat16)
    txt_b = txt_unit.astype(jnp.bfloat16)
    scale = jnp.exp(log_scale[0])
    shift = bias[0]
    block = math.gcd(PAIRS, 1024)
    count = PAIRS // block
    columns = jnp.arange(PAIRS, dtype=jnp.int32)

    def step(carry, index):
        txt_acc, scale_sum, bias_sum = carry
        begin = (index * block).astype(jnp.int32)
        left = lax.dynamic_slice_in_dim(img_b, begin, block, 0)
        cosine = jnp.dot(left, txt_b.T, preferred_element_type=jnp.float32)
        logit = scale * cosine + shift
        row_ids = begin + jnp.arange(block, dtype=jnp.int32)
        sign = jnp.where(row_ids[:, None] == columns[None, :], 1.0, -1.0).astype(jnp.float32)
        weight = -sign * jax.nn.sigmoid(-sign * logit)
        weight_b = weight.astype(jnp.bfloat16)
        img_grad_blk = scale * jnp.dot(weight_b, txt_b, preferred_element_type=jnp.float32)
        txt_acc = txt_acc + scale * jnp.dot(weight_b.T, left, preferred_element_type=jnp.float32)
        scale_sum = scale_sum + jnp.sum(weight * scale * cosine)
        bias_sum = bias_sum + jnp.sum(weight)
        return ((txt_acc, scale_sum, bias_sum), img_grad_blk)
    zero = jnp.zeros((), jnp.float32)
    init = (jnp.zeros((PAIRS, D), jnp.float32), zero, zero)
    carry, blocks = lax.scan(step, init, jnp.arange(count, dtype=jnp.int32))
    txt_unit_grad, scale_sum, bias_sum = carry
    img_unit_grad = blocks.reshape(PAIRS, D)
    image_grad = (img_unit_grad - img_unit * lax.optimization_barrier(jnp.sum(img_unit * img_unit_grad, axis=1, keepdims=True))) * inv_img
    text_grad = (txt_unit_grad - txt_unit * lax.optimization_barrier(jnp.sum(txt_unit * txt_unit_grad, axis=1, keepdims=True))) * inv_txt
    statistics = jnp.stack([scale_sum, bias_sum]).astype(jnp.float32)
    return (image_grad, text_grad, statistics)
```

```python
import jax
import jax.numpy as jnp
from jax import lax
from jax.experimental import pallas as pl
from jax.experimental.pallas import tpu as pltpu
from jax.sharding import PartitionSpec as P

D = 1152
ROWS = 12
PAD = 16
X, Y, Z = 4, 8, 16
Y_OFF = (0, 1, -1, 2, -2, 3, -3, 4)
Z_NEAR = (0, -1, 1, -2)
Z_FAR = (0, 4, -4, 8)
NX, NY, NN, NF = len(range(X)), len(Y_OFF), len(Z_NEAR), len(Z_FAR)
L_OWN = NN * NF * PAD
R_OWN = NX * NY * PAD
COLUMNS = ((0, 384), (384, 384), (768, 384))
NC = len(COLUMNS)
Y_GROUPS = ((0, 1), (1, 3), (3, 5), (5, 8))
F_GROUPS = ((0, 1), (1, 3), (3, 4))
MESH = pl.DeviceIdType.MESH
F32, BF16 = jnp.float32, jnp.bfloat16


def slot(offsets, size, offset):
    return [o % size for o in offsets].index(offset % size)


def kernel(
    img_ref, txt_ref, ls_ref, bias_ref, ig_ref, tg_ref, st_ref,
    lall, rall, cosb, wt, wb, tp, tx, ty, ip, iz, iw, stat, stat_in, send_sem, recv_sem,
):
    dp, group = lax.axis_index("dp"), lax.axis_index("group")
    zh, xx, yy = dp % 2, (dp // 2) % X, dp // (2 * X)
    zz, cc = zh * 8 + group // 2, group % 2

    def at(dx=0, dy=0, dz=0, dc=0):
        x, y, z, c = (xx + dx + X) % X, (yy + dy + Y) % Y, (zz + dz + Z) % Z, (cc + dc) % 2
        return ((y * X + x) * 2 + z // 8, (z % 8) * 2 + c)

    partners = [at(dx=d) for d in range(1, X)] + [at(dy=d) for d in Y_OFF[1:]]
    partners += [at(dz=d) for d in (1, -1, 2, -2, 4, -4, 8)] + [at(dc=1)]
    barrier = pltpu.get_barrier_semaphore()
    for p in partners:
        pl.semaphore_signal(barrier, inc=1, device_id=p, device_id_type=MESH)

    copies = []

    def send(src, dst, device):
        k = len(copies)
        copy = pltpu.make_async_remote_copy(
            src_ref=src, dst_ref=dst, send_sem=send_sem.at[k], recv_sem=recv_sem.at[k],
            device_id=device, device_id_type=MESH,
        )
        copy.start()
        copies.append(copy)
        return copy

    def unit(ref):
        full = ref[...].astype(F32)
        inverse = lax.rsqrt(jnp.sum(full * full, axis=1, keepdims=True) + 1e-06)
        return full * inverse, inverse

    for ref, own in ((img_ref, lall.at[0, 0, 0]), (txt_ref, rall.at[0, 0, 0])):
        own[...] = jnp.zeros((PAD, D), BF16)
        own[0:ROWS, :] = unit(ref)[0].astype(BF16)
    pl.semaphore_wait(barrier, len(partners))

    z_far = {}
    for f in (3, 1, 2):
        z_far[f] = send(lall.at[0, 0, 0], lall.at[0, 0, slot(Z_FAR, Z, -Z_FAR[f])], at(dz=Z_FAR[f]))
    y_got = {}
    for j in (7, 5, 6, 3, 4, 1, 2):
        to = slot(Y_OFF, Y, -Y_OFF[j])
        y_got[to] = send(rall.at[0, 0, 0], rall.at[0, 0, to], at(dy=Y_OFF[j]))
    x_got, n_got = [], []

    def x_send(lo, hi):
        for d in (2, 1, 3):
            part = pl.ds(lo, hi - lo)
            x_got.append(send(rall.at[0, 0, part], rall.at[0, X - d, part], at(dx=d)))

    def n_send(lo, hi):
        for n in (3, 1, 2):
            part = pl.ds(lo, hi - lo)
            n_got.append(send(lall.at[0, 0, part], lall.at[0, n, part], at(dz=-Z_NEAR[n])))

    far_slot = {slot(Z_FAR, Z, -Z_FAR[f]): z_far[f] for f in z_far}
    n_send(0, 1)
    x_send(0, 1)
    for lo, hi in Y_GROUPS[1:3]:
        for j in range(lo, hi):
            y_got[j].wait_recv()
        x_send(lo, hi)
    for f in (1, 2):
        far_slot[f].wait_recv()
    n_send(1, 3)
    for j in range(5, 8):
        y_got[j].wait_recv()
    x_send(5, 8)
    shared = [send(rall.at[0, 0], rall.at[1, 0], at(dc=1))]
    far_slot[3].wait_recv()
    n_send(3, 4)
    shared.append(send(lall.at[0, 0], lall.at[1, 0], at(dc=1)))
    for i, d in enumerate((2, 1, 3)):
        for copy in x_got[i::3]:
            copy.wait_recv()
        shared.append(send(rall.at[0, X - d], rall.at[1, X - d], at(dc=1)))
    for i, n in enumerate((3, 1, 2)):
        for copy in n_got[i::3]:
            copy.wait_recv()
        shared.append(send(lall.at[0, n], lall.at[1, n], at(dc=1)))
    for copy in shared:
        copy.wait_recv()

    scale = jnp.exp(jnp.full((1, 1), ls_ref[0], F32))
    shift = jnp.full((1, 1), bias_ref[0], F32)
    dims = (((1,), (1,)), ((), ()))

    def sigmoid(logit):
        return 1.0 / (1.0 + jnp.exp(-logit))

    left = lall.reshape(2 * L_OWN, D)
    right = rall.reshape(2 * R_OWN, D)
    cosb[...] = lax.dot_general(right[0:R_OWN, :], left[...], dims, preferred_element_type=F32)
    step = 64
    row_ok = lax.broadcasted_iota(jnp.int32, (step, 2 * L_OWN), 0) % PAD < ROWS
    col_ok = lax.broadcasted_iota(jnp.int32, (step, 2 * L_OWN), 1) % PAD < ROWS
    ok = jnp.where(row_ok & col_ok, 1.0, 0.0).astype(F32)

    def fold(a):
        return jnp.sum(a.reshape(step // 8, 8, a.shape[1]), axis=0)

    def weigh(i, sums):
        part = pl.ds(pl.multiple_of(i * step, step), step)
        cosine = cosb[part, :]
        weight = sigmoid(scale * cosine + shift)
        wt[part, :] = weight.astype(BF16)
        return sums[0] + fold(weight * cosine), sums[1] + fold(weight * ok)

    zero = jnp.zeros((8, 2 * L_OWN), F32)
    sum_scale, sum_bias = lax.fori_loop(0, R_OWN // step, weigh, (zero, zero))

    def lanes(a):
        return sum(a[:, 128 * i : 128 * (i + 1)] for i in range(a.shape[1] // 128))

    rows16 = lax.broadcasted_iota(jnp.int32, (PAD, 128), 0)
    cols16 = lax.broadcasted_iota(jnp.int32, (PAD, 128), 1)
    diagonal = rows16 == cols16
    counted = jnp.where(diagonal & (rows16 < ROWS), 1.0, 0.0).astype(F32)
    cosine = cosb[0:PAD, 0:128]
    logit = scale * cosine + shift
    other = sigmoid(logit)
    same = -sigmoid(-logit)
    wt[0:PAD, 0:128] = jnp.where(diagonal, same, other).astype(BF16)
    change = (same - other) * counted
    change_scale = change * cosine
    stat[0, 0:8, :] = (lanes(sum_scale) + change_scale[0:8] + change_scale[8:16]) * scale
    stat[0, 8:16, :] = lanes(sum_bias) + change[0:8] + change[8:16]

    def stat_send(level, devices):
        return [send(stat.at[level], stat_in.at[level, i], d) for i, d in enumerate(devices)]

    def stat_take(level, got):
        total = stat[level]
        for i, copy in enumerate(got):
            copy.wait_recv()
            total += stat_in[level, i]
        stat[level + 1] = total

    got0 = stat_send(0, [at(dz=d) for d in Z_NEAR[1:]])

    half = 2 * R_OWN // 2
    for h in range(2):
        cosb[0:L_OWN, :] = lax.dot_general(
            left[0:L_OWN, :], right[h * half : (h + 1) * half, :], dims, preferred_element_type=F32
        )

        def weigh_b(i, carry):
            part = pl.ds(pl.multiple_of(i * step, step), step)
            wb[part, h * half : (h + 1) * half] = sigmoid(scale * cosb[part, :] + shift).astype(BF16)
            return carry

        lax.fori_loop(0, L_OWN // step, weigh_b, 0)
        if h == 0:
            logit = scale * cosb[0:PAD, 0:128] + shift
            wb[0:PAD, 0:128] = jnp.where(diagonal, -sigmoid(-logit), sigmoid(logit)).astype(BF16)

    x_in, n_in = [], []
    for k, (begin, width) in enumerate(COLUMNS):
        cols = pl.ds(begin, width)
        t = jnp.dot(wt[...], left[:, cols], preferred_element_type=F32)
        tp[k] = t.reshape(NX, NY, PAD, width)[:, :, 0:ROWS, :]
        x_in.append({d: send(tp.at[k, d], tx.at[k, d - 1], at(dx=d)) for d in (2, 1, 3)})
        m = jnp.dot(wb[...], right[:, cols], preferred_element_type=F32)
        ip[k] = m.reshape(NN, NF, PAD, width)[:, :, 0:ROWS, :]
        n_in.append({n: send(ip.at[k, n], iz.at[k, n - 1], at(dz=Z_NEAR[n])) for n in (3, 1, 2)})
    stat_take(0, got0)
    got1 = stat_send(1, [at(dz=d) for d in Z_FAR[1:]])
    f_in, y_in = [], []
    for k in range(NC):
        for n in (1, 2, 3):
            n_in[k][n].wait_recv()
        ip[k, 0] += iz[k, 0] + iz[k, 1] + iz[k, 2]
        f_in.append([send(ip.at[k, 0, f], iw.at[k, f - 1], at(dz=Z_FAR[f])) for f in (3, 1, 2)])
        for d in (1, 3, 2):
            x_in[k][d].wait_recv()
        tp[k, 0] += tx[k, 0] + tx[k, 1] + tx[k, 2]
        y_in.append([send(tp.at[k, 0, j], ty.at[k, j - 1], at(dy=Y_OFF[j])) for j in (7, 5, 6, 3, 4, 1, 2)])
        if k == 1:
            stat_take(1, got1)
            got2 = stat_send(2, [at(dx=d) for d in range(1, X)])
    stat_take(2, got2)
    got3 = stat_send(3, [at(dy=d) for d in Y_OFF[1:]])

    def back(ref, total, out_ref):
        u, inverse = unit(ref)
        grad = scale * total
        out_ref[...] = (grad - u * jnp.sum(u * grad, axis=1, keepdims=True)) * inverse

    for k in range(NC):
        for copy in f_in[k]:
            copy.wait_recv()
    parts = [ip[k, 0, 0] + iw[k, 0] + iw[k, 1] + iw[k, 2] for k in range(NC)]
    back(img_ref, jnp.concatenate(parts, axis=1), ig_ref)
    stat_take(3, got3)
    got4 = stat_send(4, [at(dc=1)])
    for k in range(NC):
        for copy in y_in[k]:
            copy.wait_recv()
    parts = []
    for k in range(NC):
        total = tp[k, 0, 0]
        for j in range(NY - 1):
            total += ty[k, j]
        parts.append(total)
    back(txt_ref, jnp.concatenate(parts, axis=1), tg_ref)
    stat_take(4, got4)
    st_ref[0] = jnp.sum(stat[5, 0:8, :])
    st_ref[1] = jnp.sum(stat[5, 8:16, :])
    for copy in copies:
        copy.wait_send()


N_COPIES = 192


def shards(images, texts, log_scale, bias):
    width = COLUMNS[0][1]
    vmem, smem = pl.BlockSpec(memory_space=pltpu.VMEM), pl.BlockSpec(memory_space=pltpu.SMEM)
    return pl.pallas_call(
        kernel,
        out_shape=(
            jax.ShapeDtypeStruct((ROWS, D), F32),
            jax.ShapeDtypeStruct((ROWS, D), F32),
            jax.ShapeDtypeStruct((2,), F32),
        ),
        in_specs=[vmem, vmem, smem, smem],
        out_specs=(vmem, vmem, smem),
        scratch_shapes=[
            pltpu.VMEM((2, NN, NF, PAD, D), BF16),
            pltpu.VMEM((2, NX, NY, PAD, D), BF16),
            pltpu.VMEM((R_OWN, 2 * L_OWN), F32),
            pltpu.VMEM((R_OWN, 2 * L_OWN), BF16),
            pltpu.VMEM((L_OWN, 2 * R_OWN), BF16),
            pltpu.VMEM((NC, NX, NY, ROWS, width), F32),
            pltpu.VMEM((NC, NX - 1, NY, ROWS, width), F32),
            pltpu.VMEM((NC, NY - 1, ROWS, width), F32),
            pltpu.VMEM((NC, NN, NF, ROWS, width), F32),
            pltpu.VMEM((NC, NN - 1, NF, ROWS, width), F32),
            pltpu.VMEM((NC, NF - 1, ROWS, width), F32),
            pltpu.VMEM((6, 16, 128), F32),
            pltpu.VMEM((5, NY - 1, 16, 128), F32),
            pltpu.SemaphoreType.DMA((N_COPIES,)),
            pltpu.SemaphoreType.DMA((N_COPIES,)),
        ],
        compiler_params=pltpu.CompilerParams(
            collective_id=0, has_side_effects=True, vmem_limit_bytes=48 * 1024 * 1024
        ),
        cost_estimate=pl.CostEstimate(flops=3 * 2 * 512 * 512 * D, bytes_accessed=1 << 20, transcendentals=1 << 20),
        name="pair_gradients",
    )(images, texts, log_scale, bias)


def solution(mesh):
    rows = P(("dp", "group"), None)
    return jax.shard_map(
        shards, mesh=mesh, in_specs=(rows, rows, P(), P()), out_specs=(rows, rows, P()), check_vma=False
    )
```

```python
import jax
import jax.numpy as jnp
from jax import lax
from jax.experimental import pallas as pl
from jax.experimental.pallas import tpu as pltpu
from jax.sharding import PartitionSpec as P

D = 1152
ROWS = 12
PAD = 16
X, Y, Z = 4, 8, 16
Y_OFF = (0, 1, -1, 2, -2, 3, -3, 4)
Z_NEAR = (0, 1, -1)
Z_FAR = (0, 8, 4, -4)
Z_LAST = (2, -6, -2, 6)
NX, NY, NN, NF = 4, 8, 4, 4
L_OWN, R_OWN = NN * NF * PAD, NX * NY * PAD
XR, ZR = NY * ROWS, NF * ROWS
WIDTH = 384
NC = D // WIDTH
MESH = pl.DeviceIdType.MESH
F32, BF16 = jnp.float32, jnp.bfloat16
STEP = 64
N_COPIES = 160


def slot(offsets, size, offset):
    return [o % size for o in offsets].index(offset % size)


def window(entry):
    return pl.ds(24 * (entry // 2) + 8 * (entry % 2), PAD)


def kernel(
    img_hbm, txt_hbm, ls_ref, bias_ref, ig_ref, tg_ref, st_ref,
    img_ref, txt_ref, lall, rall, cosb, wt, wb, wtc, wbc, sel, tp, tx1, tx2, ty, ip, iz1, iz2, iw,
    stat, stat_in, load_sem, send_sem, recv_sem,
):
    dp, group = lax.axis_index("dp"), lax.axis_index("group")
    zh, xx, yy = dp % 2, (dp // 2) % X, dp // (2 * X)
    zz, cc = zh * 8 + group // 2, group % 2

    def at(dx=0, dy=0, dz=0, dc=0):
        x, y, z, c = (xx + dx + X) % X, (yy + dy + Y) % Y, (zz + dz + Z) % Z, (cc + dc) % 2
        return ((y * X + x) * 2 + z // 8, (z % 8) * 2 + c)

    loads = [
        pltpu.make_async_copy(img_hbm, img_ref, load_sem.at[0]),
        pltpu.make_async_copy(txt_hbm, txt_ref, load_sem.at[1]),
    ]
    for load in loads:
        load.start()
    partners = [at(dz=d) for d in (8, 4, -4)] + [at(dy=d) for d in Y_OFF[:0:-1]] + [at(dx=d) for d in (2, 1, 3)]
    partners += [at(dz=d) for d in (2, -2, 1, -1)] + [at(dc=1)]
    barrier = pltpu.get_barrier_semaphore()
    for p in partners:
        pl.semaphore_signal(barrier, inc=1, device_id=p, device_id_type=MESH)

    copies = []

    def send(src, dst, device):
        k = len(copies)
        copy = pltpu.make_async_remote_copy(
            src_ref=src, dst_ref=dst, send_sem=send_sem.at[k], recv_sem=recv_sem.at[k],
            device_id=device, device_id_type=MESH,
        )
        copy.start()
        copies.append(copy)
        return copy

    def wait(*got):
        for copy in got:
            copy.wait_recv()

    def unit(ref):
        full = ref[...].astype(F32)
        inverse = lax.rsqrt(jnp.sum(full * full, axis=1, keepdims=True) + 1e-06)
        return full * inverse, inverse

    for load, ref, own in zip(loads, (img_ref, txt_ref), (lall.at[0, 0, 0], rall.at[0, 0, 0])):
        load.wait()
        own[...] = jnp.zeros((PAD, D), BF16)
        own[0:ROWS, :] = unit(ref)[0].astype(BF16)
    r = lax.broadcasted_iota(jnp.int32, sel.shape, 0)
    c = lax.broadcasted_iota(jnp.int32, sel.shape, 1)
    picked = ((c & 15) < ROWS) & ((c >> 4) * ROWS + (c & 15) == r)
    sel[...] = jnp.where(picked, 1.0, 0.0).astype(BF16)
    pl.semaphore_wait(barrier, len(partners))

    img_own, txt_own = lall.at[0, 0], rall.at[0, 0]
    z_got, y_got = {}, {}
    for f in (1, 2, 3):
        to = slot(Z_FAR, Z, -Z_FAR[f])
        z_got[to] = send(img_own.at[0], img_own.at[to], at(dz=Z_FAR[f]))
    for j in (7, 5, 6, 3, 4, 1, 2):
        to = slot(Y_OFF, Y, -Y_OFF[j])
        y_got[to] = send(txt_own.at[0], txt_own.at[to], at(dy=Y_OFF[j]))

    def x_send(lo, hi, straight=False):
        part = pl.ds(lo, hi - lo)
        got = {}
        if straight:
            got[2] = send(txt_own.at[part], rall.at[0, 2, part], at(dx=2))
        got[3] = send(txt_own.at[part], rall.at[0, 3, part], at(dx=1))
        got[1] = send(txt_own.at[part], rall.at[0, 1, part], at(dx=-1))
        return got

    def x_relay(got, frm, lo, hi):
        part = pl.ds(lo, hi - lo)
        wait(got[frm])
        got[2] = send(rall.at[0, frm, part], rall.at[0, 2, part], at(dx=1 if frm == 3 else -1))

    def n_send(lo, hi):
        part = pl.ds(lo, hi - lo)
        return {
            2: send(img_own.at[part], lall.at[0, 2, part], at(dz=1)),
            1: send(img_own.at[part], lall.at[0, 1, part], at(dz=-1)),
        }

    def n_relay(frm, entry):
        offset = Z_NEAR[frm] * 2 + Z_FAR[entry]
        to = slot(Z_LAST, Z, offset)
        return send(lall.at[0, frm, entry], lall.at[0, 3, to], at(dz=-Z_NEAR[frm]))

    n0 = n_send(0, 1)
    x0 = x_send(0, 1)
    wait(y_got[1], y_got[2])
    x1 = x_send(1, 3)
    wait(n0[1], n0[2])
    last = [n_relay(1, 0), n_relay(2, 0)]
    x_relay(x0, 3, 0, 1)
    wait(y_got[3], y_got[4])
    x2 = x_send(3, 5)
    wait(z_got[2], z_got[3])
    n1 = n_send(2, 4)
    x_relay(x1, 1, 1, 3)
    wait(y_got[5], y_got[6], y_got[7])
    x3 = x_send(5, 8, straight=True)
    shared_r = [send(rall.at[0, 0], rall.at[1, 0], at(dc=1))]
    x_relay(x2, 3, 3, 5)
    wait(n1[1], n1[2])
    last += [n_relay(1, 2), n_relay(2, 3)]
    wait(z_got[1])
    n2 = n_send(1, 2)
    shared_l = [send(lall.at[0, 0], lall.at[1, 0], at(dc=1))]
    wait(x0[1], x1[3], x2[1])
    for s in (3, 1, 2):
        wait(x3[s])
        if s == 2:
            wait(x0[2], x1[2], x2[2])
        shared_r.append(send(rall.at[0, s], rall.at[1, s], at(dc=1)))
    for s in (2, 1):
        wait(n2[s])
        shared_l.append(send(lall.at[0, s], lall.at[1, s], at(dc=1)))
    wait(*last)
    shared_l.append(send(lall.at[0, 3], lall.at[1, 3], at(dc=1)))

    scale = jnp.exp(jnp.full((1, 1), ls_ref[0], F32))
    shift = jnp.full((1, 1), bias_ref[0], F32)
    dims = (((1,), (1,)), ((), ()))

    def sigmoid(logit):
        return 1.0 / (1.0 + jnp.exp(-logit))

    def row_blocks(core, ref, n):
        return ref.at[core].reshape(n, D)

    left = [row_blocks(i, lall, L_OWN) for i in range(2)]
    right = [row_blocks(i, rall, R_OWN) for i in range(2)]
    row_ok = (lax.broadcasted_iota(jnp.int32, (STEP, L_OWN), 0) & 15) < ROWS
    col_ok = (lax.broadcasted_iota(jnp.int32, (STEP, L_OWN), 1) & 15) < ROWS
    ok = jnp.where(row_ok & col_ok, 1.0, 0.0).astype(F32)

    def fold(a):
        return jnp.sum(a.reshape(STEP // 8, 8, a.shape[1]), axis=0)

    def text_weights(core, sums):
        cosb[:, 0:L_OWN] = lax.dot_general(right[0][...], left[core][...], dims, preferred_element_type=F32)
        cols = slice(core * L_OWN, (core + 1) * L_OWN)

        def weigh(i, sums):
            part = pl.ds(pl.multiple_of(i * STEP, STEP), STEP)
            cosine = cosb[part, 0:L_OWN]
            weight = sigmoid(scale * cosine + shift)
            wt[part, cols] = weight.astype(BF16)
            return sums[0] + fold(weight * cosine), sums[1] + fold(weight * ok)

        return lax.fori_loop(0, R_OWN // STEP, weigh, sums)

    def image_weights(core):
        cosb[0:L_OWN, :] = lax.dot_general(left[0][...], right[core][...], dims, preferred_element_type=F32)
        cols = slice(core * R_OWN, (core + 1) * R_OWN)

        def weigh(i, carry):
            part = pl.ds(pl.multiple_of(i * STEP, STEP), STEP)
            wb[part, cols] = sigmoid(scale * cosb[part, :] + shift).astype(BF16)
            return carry

        lax.fori_loop(0, L_OWN // STEP, weigh, 0)

    def lanes(a):
        return sum(a[:, 128 * i : 128 * (i + 1)] for i in range(a.shape[1] // 128))

    rows16 = lax.broadcasted_iota(jnp.int32, (PAD, 128), 0)
    cols16 = lax.broadcasted_iota(jnp.int32, (PAD, 128), 1)
    diagonal = rows16 == cols16
    counted = jnp.where(diagonal & (rows16 < ROWS), 1.0, 0.0).astype(F32)

    zero = jnp.zeros((8, L_OWN), F32)
    sums = text_weights(0, (zero, zero))
    cosine = cosb[0:PAD, 0:128]
    logit = scale * cosine + shift
    other, same = sigmoid(logit), -sigmoid(-logit)
    wt[0:PAD, 0:128] = jnp.where(diagonal, same, other).astype(BF16)
    change = (same - other) * counted
    change_scale = change * cosine
    wait(*shared_l)
    sums = text_weights(1, sums)
    stat[0, 0:8, :] = (lanes(sums[0]) + change_scale[0:8] + change_scale[8:16]) * scale
    stat[0, 8:16, :] = lanes(sums[1]) + change[0:8] + change[8:16]

    def stat_send(level, devices):
        return [send(stat.at[level], stat_in.at[level, i], d) for i, d in enumerate(devices)]

    def stat_take(level, got):
        wait(*got)
        total = stat[level]
        for i in range(len(got)):
            total += stat_in[level, i]
        stat[level + 1] = total

    stat_got = stat_send(0, [at(dz=d) for d in Z_FAR[1:]])
    wtc[...] = jnp.dot(sel[...], wt[...], preferred_element_type=F32).astype(BF16)

    def cols_of(k):
        return pl.ds(k * WIDTH, WIDTH)

    x_in, z_in = {}, {}

    def text_part(k):
        t = jnp.dot(wtc[:, 0:L_OWN], left[0][:, cols_of(k)], preferred_element_type=F32)
        t += jnp.dot(wtc[:, L_OWN : 2 * L_OWN], left[1][:, cols_of(k)], preferred_element_type=F32)
        tp[k] = t.reshape(NX, XR, WIDTH)
        x_in[k] = [
            send(tp.at[k, 2, pl.ds(0, XR // 2)], tx1.at[k, 0], at(dx=1)),
            send(tp.at[k, 2, pl.ds(XR // 2, XR // 2)], tx1.at[k, 1], at(dx=-1)),
        ]

    def image_part(k):
        m = jnp.dot(wbc[:, 0:R_OWN], right[0][:, cols_of(k)], preferred_element_type=F32)
        m += jnp.dot(wbc[:, R_OWN : 2 * R_OWN], right[1][:, cols_of(k)], preferred_element_type=F32)
        ip[k] = m.reshape(NN, ZR, WIDTH)
        z_in[k] = [
            send(ip.at[k, 3, pl.ds(0, ZR // 2)], iz1.at[k, 0], at(dz=1)),
            send(ip.at[k, 3, pl.ds(ZR // 2, ZR // 2)], iz1.at[k, 1], at(dz=-1)),
        ]

    text_part(0)
    image_weights(0)
    logit = scale * cosb[0:PAD, 0:128] + shift
    wb[0:PAD, 0:128] = jnp.where(diagonal, -sigmoid(-logit), sigmoid(logit)).astype(BF16)
    wait(*shared_r)
    image_weights(1)
    wbc[...] = jnp.dot(sel[0 : NN * ZR, 0:L_OWN], wb[...], preferred_element_type=F32).astype(BF16)
    image_part(0)
    for k in range(1, NC):
        text_part(k)
        image_part(k)

    f_in, y_in = {}, {}
    for k in range(NC):
        wait(*x_in[k])
        tp[k, 1, 0 : XR // 2] += tx1[k, 0]
        tp[k, 3, XR // 2 : XR] += tx1[k, 1]
        x_in[k] = [send(tp.at[k, 1], tx2.at[k, 0], at(dx=1)), send(tp.at[k, 3], tx2.at[k, 1], at(dx=-1))]
        wait(*z_in[k])
        ip[k, 1, 0 : ZR // 2] += iz1[k, 0]
        ip[k, 2, 0 : ZR // 2] += iz1[k, 1]
        z_in[k] = [send(ip.at[k, 1], iz2.at[k, 0], at(dz=1)), send(ip.at[k, 2], iz2.at[k, 1], at(dz=-1))]
    stat_take(0, stat_got)
    stat_got = stat_send(1, [at(dy=d) for d in Y_OFF[1:]])
    for k in range(NC):
        wait(*z_in[k])
        ip[k, 0] += iz2[k, 0] + iz2[k, 1]
        f_in[k] = [send(ip.at[k, 0, window(f)], iw.at[k, f - 1], at(dz=Z_FAR[f])) for f in (1, 2, 3)]
        wait(*x_in[k])
        tp[k, 0] += tx2[k, 0] + tx2[k, 1]
        y_in[k] = [send(tp.at[k, 0, window(j)], ty.at[k, j - 1], at(dy=Y_OFF[j])) for j in (7, 5, 6, 3, 4, 1, 2)]
        if k == 0:
            stat_take(1, stat_got)
            stat_got = stat_send(2, [at(dx=d) for d in (1, 2, 3)])
    stat_take(2, stat_got)
    stat_got = stat_send(3, [at(dz=d) for d in (2, 1, -1)])

    def total_of(own, ref, k, n):
        even, odd = own, None
        for e in range(1, n):
            got = ref[k, e - 1]
            if e % 2 == 0:
                even = even + got
            else:
                odd = got if odd is None else odd + got
        return even[0:ROWS] + odd[PAD - ROWS : PAD]

    def back(ref, total, out_ref):
        u, inverse = unit(ref)
        grad = scale * total
        out_ref[...] = (grad - u * jnp.sum(u * grad, axis=1, keepdims=True)) * inverse

    for k in range(NC):
        wait(*f_in[k])
    back(img_ref, jnp.concatenate([total_of(ip[k, 0, 0:PAD], iw, k, NF) for k in range(NC)], axis=1), ig_ref)
    stat_take(3, stat_got)
    stat_got = stat_send(4, [at(dc=1)])
    for k in range(NC):
        wait(*y_in[k])
    back(txt_ref, jnp.concatenate([total_of(tp[k, 0, 0:PAD], ty, k, NY) for k in range(NC)], axis=1), tg_ref)
    stat_take(4, stat_got)
    st_ref[0] = jnp.sum(stat[5, 0:8, :])
    st_ref[1] = jnp.sum(stat[5, 8:16, :])
    for copy in copies:
        copy.wait_send()


def shards(images, texts, log_scale, bias):
    vmem, smem = pl.BlockSpec(memory_space=pltpu.VMEM), pl.BlockSpec(memory_space=pltpu.SMEM)
    hbm = pl.BlockSpec(memory_space=pltpu.HBM)
    return pl.pallas_call(
        kernel,
        out_shape=(
            jax.ShapeDtypeStruct((ROWS, D), F32),
            jax.ShapeDtypeStruct((ROWS, D), F32),
            jax.ShapeDtypeStruct((2,), F32),
        ),
        in_specs=[hbm, hbm, smem, smem],
        out_specs=(vmem, vmem, smem),
        scratch_shapes=[
            pltpu.VMEM((ROWS, D), BF16),
            pltpu.VMEM((ROWS, D), BF16),
            pltpu.VMEM((2, NN, NF, PAD, D), BF16),
            pltpu.VMEM((2, NX, NY, PAD, D), BF16),
            pltpu.VMEM((R_OWN, R_OWN), F32),
            pltpu.VMEM((R_OWN, 2 * L_OWN), BF16),
            pltpu.VMEM((L_OWN, 2 * R_OWN), BF16),
            pltpu.VMEM((NX * XR, 2 * L_OWN), BF16),
            pltpu.VMEM((NN * ZR, 2 * R_OWN), BF16),
            pltpu.VMEM((NX * XR, R_OWN), BF16),
            pltpu.VMEM((NC, NX, XR, WIDTH), F32),
            pltpu.VMEM((NC, 2, XR // 2, WIDTH), F32),
            pltpu.VMEM((NC, 2, XR, WIDTH), F32),
            pltpu.VMEM((NC, NY - 1, PAD, WIDTH), F32),
            pltpu.VMEM((NC, NN, ZR, WIDTH), F32),
            pltpu.VMEM((NC, 2, ZR // 2, WIDTH), F32),
            pltpu.VMEM((NC, 2, ZR, WIDTH), F32),
            pltpu.VMEM((NC, NF - 1, PAD, WIDTH), F32),
            pltpu.VMEM((6, 16, 128), F32),
            pltpu.VMEM((5, NY - 1, 16, 128), F32),
            pltpu.SemaphoreType.DMA((2,)),
            pltpu.SemaphoreType.DMA((N_COPIES,)),
            pltpu.SemaphoreType.DMA((N_COPIES,)),
        ],
        compiler_params=pltpu.CompilerParams(
            collective_id=0, has_side_effects=True, vmem_limit_bytes=48 * 1024 * 1024
        ),
        cost_estimate=pl.CostEstimate(flops=3 * 2 * 512 * 512 * D, bytes_accessed=1 << 20, transcendentals=1 << 20),
        name="pair_gradients",
    )(images, texts, log_scale, bias)


def solution(mesh):
    rows = P(("dp", "group"), None)
    return jax.shard_map(
        shards, mesh=mesh, in_specs=(rows, rows, P(), P()), out_specs=(rows, rows, P()), check_vma=False
    )
```

```python
import jax
import jax.numpy as jnp
from jax import lax
from jax.experimental import pallas as pl
from jax.experimental.pallas import tpu as pltpu
from jax.sharding import PartitionSpec as P

D = 1152
ROWS = 12
PAD = 16
X, Y, Z = 4, 8, 16
Y_OFF = (0, 1, -1, 2, -2, 3, -3, 4)
Z_NEAR = (0, 1, -1)
Z_FAR = (0, 8, 4, -4)
Z_LAST = (2, -6, -2, 6)
NX, NY, NN, NF = 4, 8, 4, 4
L_OWN, R_OWN = NN * NF * PAD, NX * NY * PAD
XR, ZR = NY * ROWS, NF * ROWS
WIDTH = 384
NC = D // WIDTH
SPLIT = 896
MESH = pl.DeviceIdType.MESH
F32, BF16 = jnp.float32, jnp.bfloat16
STEP = 64
N_COPIES = 160


def slot(offsets, size, offset):
    return [o % size for o in offsets].index(offset % size)


def window(entry):
    return pl.ds(24 * (entry // 2) + 8 * (entry % 2), PAD)


def kernel(
    img_hbm, txt_hbm, ls_ref, bias_ref, ig_ref, tg_ref, st_ref,
    img_ref, txt_ref, lall, rall, cosb, wt, wb, wtc, wbc, sel, tp, tx1, tx2, ty, ip, iz1, iz2, iw,
    stat, stat_in, load_sem, send_sem, recv_sem,
):
    dp, group = lax.axis_index("dp"), lax.axis_index("group")
    zh, xx, yy = dp % 2, (dp // 2) % X, dp // (2 * X)
    zz, cc = zh * 8 + group // 2, group % 2

    def at(dx=0, dy=0, dz=0, dc=0):
        x, y, z, c = (xx + dx + X) % X, (yy + dy + Y) % Y, (zz + dz + Z) % Z, (cc + dc) % 2
        return ((y * X + x) * 2 + z // 8, (z % 8) * 2 + c)

    loads = [
        pltpu.make_async_copy(img_hbm, img_ref, load_sem.at[0]),
        pltpu.make_async_copy(txt_hbm, txt_ref, load_sem.at[1]),
    ]
    for load in loads:
        load.start()
    partners = [at(dz=d) for d in (8, 4, -4)] + [at(dy=d) for d in Y_OFF[:0:-1]] + [at(dx=d) for d in (2, 1, 3)]
    partners += [at(dz=d) for d in (2, -2, 1, -1)] + [at(dc=1)]
    barrier = pltpu.get_barrier_semaphore()
    for p in partners:
        pl.semaphore_signal(barrier, inc=1, device_id=p, device_id_type=MESH)

    taken, unsent = [0], []

    def remote(k, src, dst, device):
        return pltpu.make_async_remote_copy(
            src_ref=src, dst_ref=dst, send_sem=send_sem.at[k], recv_sem=recv_sem.at[k],
            device_id=device, device_id_type=MESH,
        )

    def send_all(parts, whole):
        k = taken[0]
        taken[0] += 1
        for src, dst, device in parts:
            remote(k, src, dst, device).start()
        copy = remote(k, whole, whole, parts[0][2])
        unsent.append(copy)
        return copy

    def send(src, dst, device):
        return send_all([(src, dst, device)], dst)

    def wait_sent(n):
        for copy in unsent[:n]:
            copy.wait_send()
        del unsent[:n]

    def wait(*got):
        for copy in got:
            copy.wait_recv()

    def unit(ref):
        full = ref[...].astype(F32)
        inverse = lax.rsqrt(jnp.sum(full * full, axis=1, keepdims=True) + 1e-06)
        return full * inverse, inverse

    for load, ref, own in zip(loads, (img_ref, txt_ref), (lall.at[0, 0, 0], rall.at[0, 0, 0])):
        load.wait()
        own[...] = jnp.zeros((PAD, D), BF16)
        own[0:ROWS, :] = unit(ref)[0].astype(BF16)
    r = lax.broadcasted_iota(jnp.int32, sel.shape, 0)
    c = lax.broadcasted_iota(jnp.int32, sel.shape, 1)
    picked = ((c & 15) < ROWS) & ((c >> 4) * ROWS + (c & 15) == r)
    sel[...] = jnp.where(picked, 1.0, 0.0).astype(BF16)
    pl.semaphore_wait(barrier, len(partners))

    img_own, txt_own = lall.at[0, 0], rall.at[0, 0]
    def far_first(lo, hi):
        to = [slot(Z_FAR, Z, -Z_FAR[f]) for f in range(lo, hi)]
        parts = [(img_own.at[0], img_own.at[t], at(dz=Z_FAR[f])) for t, f in zip(to, range(lo, hi))]
        return send_all(parts, img_own.at[pl.ds(lo, hi - lo)])

    main, rest = pl.ds(0, SPLIT), pl.ds(SPLIT, D - SPLIT)

    def y_first(*entries):
        to = [slot(Y_OFF, Y, -Y_OFF[j]) for j in entries]
        parts = [(txt_own.at[0, :, main], txt_own.at[t, :, main], at(dy=Y_OFF[j])) for t, j in zip(to, entries)]
        return send_all(parts, txt_own.at[pl.ds(min(entries), len(entries)), :, main])

    z_eight = far_first(1, 2)
    x_rest = send_all(
        [(rall.at[0, 0, 0, :, rest], rall.at[0, X - d, 0, :, rest], at(dx=d)) for d in (2, 1, 3)],
        rall.at[0, pl.ds(1, NX - 1), 0, :, rest],
    )
    y_far = y_first(7, 5, 6)
    z_four = far_first(2, 4)
    y_two, y_one = y_first(3, 4), y_first(1, 2)

    def x_send(lo, hi, straight=False):
        part = pl.ds(lo, hi - lo)
        got = {}
        if straight:
            got[2] = send(txt_own.at[part, :, main], rall.at[0, 2, part, :, main], at(dx=2))
        got[3] = send(txt_own.at[part, :, main], rall.at[0, 3, part, :, main], at(dx=1))
        got[1] = send(txt_own.at[part, :, main], rall.at[0, 1, part, :, main], at(dx=-1))
        return got

    def x_relay(got, frm, lo, hi):
        part = pl.ds(lo, hi - lo)
        wait(got[frm])
        to = at(dx=1 if frm == 3 else -1)
        got[2] = send(rall.at[0, frm, part, :, main], rall.at[0, 2, part, :, main], to)

    def n_send(lo, hi):
        part = pl.ds(lo, hi - lo)
        return {
            2: send(img_own.at[part], lall.at[0, 2, part], at(dz=1)),
            1: send(img_own.at[part], lall.at[0, 1, part], at(dz=-1)),
        }

    def n_relay(frm, entry):
        offset = Z_NEAR[frm] * 2 + Z_FAR[entry]
        to = slot(Z_LAST, Z, offset)
        return send(lall.at[0, frm, entry], lall.at[0, 3, to], at(dz=-Z_NEAR[frm]))

    n0 = n_send(0, 1)
    x0 = x_send(0, 1)
    wait(x_rest)
    near = [(j, slot(Y_OFF, Y, -Y_OFF[j])) for j in (7, 5, 6, 3, 4, 1, 2)]
    y_rest = send_all(
        [(rall.at[0, :, 0, :, rest], rall.at[0, :, t, :, rest], at(dy=Y_OFF[j])) for j, t in near],
        rall.at[0, :, pl.ds(1, NY - 1), :, rest],
    )
    wait(y_one)
    x1 = x_send(1, 3)
    wait(n0[1], n0[2])
    last = [n_relay(1, 0), n_relay(2, 0)]
    x_relay(x0, 3, 0, 1)
    wait(y_two)
    x2 = x_send(3, 5)
    wait(z_four)
    n1 = n_send(2, 4)
    x_relay(x1, 1, 1, 3)
    wait(y_far)
    x3 = x_send(5, 8, straight=True)
    x_relay(x2, 3, 3, 5)
    wait(n1[1], n1[2])
    last += [n_relay(1, 2), n_relay(2, 3)]
    wait(z_eight)
    n2 = n_send(1, 2)
    shared_l = [send(lall.at[0, 0], lall.at[1, 0], at(dc=1))]
    wait(x0[1], x1[3], x2[1])
    wait(y_rest)
    shared_r = [send(rall.at[0, 0], rall.at[1, 0], at(dc=1))]
    for s in (3, 1, 2):
        wait(x3[s])
        if s == 2:
            wait(x0[2], x1[2], x2[2])
        shared_r.append(send(rall.at[0, s], rall.at[1, s], at(dc=1)))
    for s in (2, 1):
        wait(n2[s])
        shared_l.append(send(lall.at[0, s], lall.at[1, s], at(dc=1)))
    wait(*last)
    shared_l.append(send(lall.at[0, 3], lall.at[1, 3], at(dc=1)))

    scale = jnp.exp(jnp.full((1, 1), ls_ref[0], F32))
    shift = jnp.full((1, 1), bias_ref[0], F32)
    dims = (((1,), (1,)), ((), ()))

    def sigmoid(logit):
        return 1.0 / (1.0 + jnp.exp(-logit))

    def row_blocks(core, ref, n):
        return ref.at[core].reshape(n, D)

    left = [row_blocks(i, lall, L_OWN) for i in range(2)]
    right = [row_blocks(i, rall, R_OWN) for i in range(2)]
    row_ok = (lax.broadcasted_iota(jnp.int32, (STEP, L_OWN), 0) & 15) < ROWS
    col_ok = (lax.broadcasted_iota(jnp.int32, (STEP, L_OWN), 1) & 15) < ROWS
    ok = jnp.where(row_ok & col_ok, 1.0, 0.0).astype(F32)

    def fold(a):
        return jnp.sum(a.reshape(STEP // 8, 8, a.shape[1]), axis=0)

    def text_weights(core, sums):
        cosb[:, 0:L_OWN] = lax.dot_general(right[0][...], left[core][...], dims, preferred_element_type=F32)
        cols = slice(core * L_OWN, (core + 1) * L_OWN)

        def weigh(i, sums):
            part = pl.ds(pl.multiple_of(i * STEP, STEP), STEP)
            cosine = cosb[part, 0:L_OWN]
            weight = sigmoid(scale * cosine + shift)
            wt[part, cols] = weight.astype(BF16)
            return sums[0] + fold(weight * cosine), sums[1] + fold(weight * ok)

        return lax.fori_loop(0, R_OWN // STEP, weigh, sums)

    def image_weights(core):
        cosb[0:L_OWN, :] = lax.dot_general(left[0][...], right[core][...], dims, preferred_element_type=F32)
        cols = slice(core * R_OWN, (core + 1) * R_OWN)

        def weigh(i, carry):
            part = pl.ds(pl.multiple_of(i * STEP, STEP), STEP)
            wb[part, cols] = sigmoid(scale * cosb[part, :] + shift).astype(BF16)
            return carry

        lax.fori_loop(0, L_OWN // STEP, weigh, 0)

    def lanes(a):
        return sum(a[:, 128 * i : 128 * (i + 1)] for i in range(a.shape[1] // 128))

    rows16 = lax.broadcasted_iota(jnp.int32, (PAD, 128), 0)
    cols16 = lax.broadcasted_iota(jnp.int32, (PAD, 128), 1)
    diagonal = rows16 == cols16
    counted = jnp.where(diagonal & (rows16 < ROWS), 1.0, 0.0).astype(F32)

    zero = jnp.zeros((8, L_OWN), F32)
    sums = text_weights(0, (zero, zero))
    cosine = cosb[0:PAD, 0:128]
    logit = scale * cosine + shift
    other, same = sigmoid(logit), -sigmoid(-logit)
    wt[0:PAD, 0:128] = jnp.where(diagonal, same, other).astype(BF16)
    change = (same - other) * counted
    change_scale = change * cosine
    wait(*shared_l)
    sums = text_weights(1, sums)
    stat[0, 0:8, :] = (lanes(sums[0]) + change_scale[0:8] + change_scale[8:16]) * scale
    stat[0, 8:16, :] = lanes(sums[1]) + change[0:8] + change[8:16]

    def stat_send(level, devices):
        parts = [(stat.at[level], stat_in.at[level, i], d) for i, d in enumerate(devices)]
        return send_all(parts, stat_in.at[level, pl.ds(0, len(parts))])

    def stat_take(level, got, n):
        wait(got)
        total = stat[level]
        for i in range(n):
            total += stat_in[level, i]
        stat[level + 1] = total

    stat_got = stat_send(0, [at(dz=d) for d in Z_FAR[1:]])
    wtc[...] = jnp.dot(sel[...], wt[...], preferred_element_type=F32).astype(BF16)

    def cols_of(k):
        return pl.ds(k * WIDTH, WIDTH)

    x_in, z_in = {}, {}

    def text_part(k):
        t = jnp.dot(wtc[:, 0:L_OWN], left[0][:, cols_of(k)], preferred_element_type=F32)
        t += jnp.dot(wtc[:, L_OWN : 2 * L_OWN], left[1][:, cols_of(k)], preferred_element_type=F32)
        tp[k] = t.reshape(NX, XR, WIDTH)
        x_in[k] = [
            send(tp.at[k, 2, pl.ds(0, XR // 2)], tx1.at[k, 0], at(dx=1)),
            send(tp.at[k, 2, pl.ds(XR // 2, XR // 2)], tx1.at[k, 1], at(dx=-1)),
        ]

    def image_part(k):
        m = jnp.dot(wbc[:, 0:R_OWN], right[0][:, cols_of(k)], preferred_element_type=F32)
        m += jnp.dot(wbc[:, R_OWN : 2 * R_OWN], right[1][:, cols_of(k)], preferred_element_type=F32)
        ip[k] = m.reshape(NN, ZR, WIDTH)
        z_in[k] = [
            send(ip.at[k, 3, pl.ds(0, ZR // 2)], iz1.at[k, 0], at(dz=1)),
            send(ip.at[k, 3, pl.ds(ZR // 2, ZR // 2)], iz1.at[k, 1], at(dz=-1)),
        ]

    old = len(unsent)
    f_in, y_in = {}, {}

    def text_merge(k):
        wait(*x_in[k])
        tp[k, 1, 0 : XR // 2] += tx1[k, 0]
        tp[k, 3, XR // 2 : XR] += tx1[k, 1]
        x_in[k] = [send(tp.at[k, 1], tx2.at[k, 0], at(dx=1)), send(tp.at[k, 3], tx2.at[k, 1], at(dx=-1))]

    def image_merge(k):
        wait(*z_in[k])
        ip[k, 1, 0 : ZR // 2] += iz1[k, 0]
        ip[k, 2, 0 : ZR // 2] += iz1[k, 1]
        z_in[k] = [send(ip.at[k, 1], iz2.at[k, 0], at(dz=1)), send(ip.at[k, 2], iz2.at[k, 1], at(dz=-1))]

    for k in range(NC):
        text_part(k)
    image_weights(0)
    logit = scale * cosb[0:PAD, 0:128] + shift
    wb[0:PAD, 0:128] = jnp.where(diagonal, -sigmoid(-logit), sigmoid(logit)).astype(BF16)
    wait(*shared_r)
    image_weights(1)
    wbc[...] = jnp.dot(sel[0 : NN * ZR, 0:L_OWN], wb[...], preferred_element_type=F32).astype(BF16)
    for k in range(NC):
        image_part(k)
        text_merge(k)
    wait_sent(old)
    for k in range(NC):
        image_merge(k)
    stat_take(0, stat_got, NF - 1)
    old = len(unsent)
    stat_got = stat_send(1, [at(dy=d) for d in Y_OFF[1:]])
    for k in range(NC):
        wait(*z_in[k])
        ip[k, 0] += iz2[k, 0] + iz2[k, 1]
        f_in[k] = send_all([(ip.at[k, 0, window(f)], iw.at[k, f - 1], at(dz=Z_FAR[f])) for f in (1, 2, 3)], iw.at[k])
        wait(*x_in[k])
        tp[k, 0] += tx2[k, 0] + tx2[k, 1]
        y_in[k] = send_all(
            [(tp.at[k, 0, window(j)], ty.at[k, j - 1], at(dy=Y_OFF[j])) for j in (7, 5, 6, 3, 4, 1, 2)], ty.at[k]
        )
        if k == 0:
            stat_take(1, stat_got, NY - 1)
            stat_got = stat_send(2, [at(dx=d) for d in (1, 2, 3)])
    stat_take(2, stat_got, NX - 1)
    stat_got = stat_send(3, [at(dz=d) for d in (2, 1, -1)])

    wait_sent(old)

    def total_of(own, ref, k, n):
        even, odd = own, None
        for e in range(1, n):
            got = ref[k, e - 1]
            if e % 2 == 0:
                even = even + got
            else:
                odd = got if odd is None else odd + got
        return even[0:ROWS] + odd[PAD - ROWS : PAD]

    def back(ref, total, out_ref):
        u, inverse = unit(ref)
        grad = scale * total
        out_ref[...] = (grad - u * jnp.sum(u * grad, axis=1, keepdims=True)) * inverse

    for k in range(NC):
        wait(f_in[k])
    back(img_ref, jnp.concatenate([total_of(ip[k, 0, 0:PAD], iw, k, NF) for k in range(NC)], axis=1), ig_ref)
    stat_take(3, stat_got, 3)
    stat_got = stat_send(4, [at(dc=1)])
    for k in range(NC):
        wait(y_in[k])
    back(txt_ref, jnp.concatenate([total_of(tp[k, 0, 0:PAD], ty, k, NY) for k in range(NC)], axis=1), tg_ref)
    stat_take(4, stat_got, 1)
    st_ref[0] = jnp.sum(stat[5, 0:8, :])
    st_ref[1] = jnp.sum(stat[5, 8:16, :])
    wait_sent(len(unsent))


def shards(images, texts, log_scale, bias):
    vmem, smem = pl.BlockSpec(memory_space=pltpu.VMEM), pl.BlockSpec(memory_space=pltpu.SMEM)
    hbm = pl.BlockSpec(memory_space=pltpu.HBM)
    return pl.pallas_call(
        kernel,
        out_shape=(
            jax.ShapeDtypeStruct((ROWS, D), F32),
            jax.ShapeDtypeStruct((ROWS, D), F32),
            jax.ShapeDtypeStruct((2,), F32),
        ),
        in_specs=[hbm, hbm, smem, smem],
        out_specs=(vmem, vmem, smem),
        scratch_shapes=[
            pltpu.VMEM((ROWS, D), BF16),
            pltpu.VMEM((ROWS, D), BF16),
            pltpu.VMEM((2, NN, NF, PAD, D), BF16),
            pltpu.VMEM((2, NX, NY, PAD, D), BF16),
            pltpu.VMEM((R_OWN, R_OWN), F32),
            pltpu.VMEM((R_OWN, 2 * L_OWN), BF16),
            pltpu.VMEM((L_OWN, 2 * R_OWN), BF16),
            pltpu.VMEM((NX * XR, 2 * L_OWN), BF16),
            pltpu.VMEM((NN * ZR, 2 * R_OWN), BF16),
            pltpu.VMEM((NX * XR, R_OWN), BF16),
            pltpu.VMEM((NC, NX, XR, WIDTH), F32),
            pltpu.VMEM((NC, 2, XR // 2, WIDTH), F32),
            pltpu.VMEM((NC, 2, XR, WIDTH), F32),
            pltpu.VMEM((NC, NY - 1, PAD, WIDTH), F32),
            pltpu.VMEM((NC, NN, ZR, WIDTH), F32),
            pltpu.VMEM((NC, 2, ZR // 2, WIDTH), F32),
            pltpu.VMEM((NC, 2, ZR, WIDTH), F32),
            pltpu.VMEM((NC, NF - 1, PAD, WIDTH), F32),
            pltpu.VMEM((6, 16, 128), F32),
            pltpu.VMEM((5, NY - 1, 16, 128), F32),
            pltpu.SemaphoreType.DMA((2,)),
            pltpu.SemaphoreType.DMA((N_COPIES,)),
            pltpu.SemaphoreType.DMA((N_COPIES,)),
        ],
        compiler_params=pltpu.CompilerParams(
            collective_id=0, has_side_effects=True, vmem_limit_bytes=48 * 1024 * 1024
        ),
        cost_estimate=pl.CostEstimate(flops=3 * 2 * 512 * 512 * D, bytes_accessed=1 << 20, transcendentals=1 << 20),
        name="pair_gradients",
    )(images, texts, log_scale, bias)


def solution(mesh):
    rows = P(("dp", "group"), None)
    return jax.shard_map(
        shards, mesh=mesh, in_specs=(rows, rows, P(), P()), out_specs=(rows, rows, P()), check_vma=False
    )
```

```python
import jax
import jax.numpy as jnp
from jax import lax
from jax.experimental import pallas as pl
from jax.experimental.pallas import tpu as pltpu
from jax.sharding import PartitionSpec as P

D = 1152
ROWS = 12
PAD = 16
X, Y, Z = 4, 8, 16
Y_OFF = (0, 1, -1, 2, -2, 3, -3, 4)
Z_NEAR = (0, 1, -1)
Z_FAR = (0, 8, 4, -4)
Z_LAST = (2, -6, -2, 6)
NX, NY, NN, NF = 4, 8, 4, 4
L_OWN, R_OWN = NN * NF * PAD, NX * NY * PAD
XR, ZR = NY * ROWS, NF * ROWS
WIDTH = 384
NC = D // WIDTH
SPLIT = 896
MESH = pl.DeviceIdType.MESH
F32, BF16 = jnp.float32, jnp.bfloat16
STEP = 64
N_COPIES = 160


def slot(offsets, size, offset):
    return [o % size for o in offsets].index(offset % size)


def window(entry):
    return pl.ds(24 * (entry // 2) + 8 * (entry % 2), PAD)


def kernel(
    img_hbm, txt_hbm, ls_ref, bias_ref, ig_ref, tg_ref, st_ref,
    img_ref, txt_ref, lall, rall, cosb, wt, wb, wtc, wbc, sel, tp, tx1, tx2, ty, ip, iz1, iz2, iw, fb,
    stat, stat_in, load_sem, send_sem, recv_sem,
):
    dp, group = lax.axis_index("dp"), lax.axis_index("group")
    zh, xx, yy = dp % 2, (dp // 2) % X, dp // (2 * X)
    zz, cc = zh * 8 + group // 2, group % 2

    def at(dx=0, dy=0, dz=0, dc=0):
        x, y, z, c = (xx + dx + X) % X, (yy + dy + Y) % Y, (zz + dz + Z) % Z, (cc + dc) % 2
        return ((y * X + x) * 2 + z // 8, (z % 8) * 2 + c)

    loads = [
        pltpu.make_async_copy(img_hbm, img_ref, load_sem.at[0]),
        pltpu.make_async_copy(txt_hbm, txt_ref, load_sem.at[1]),
    ]
    for load in loads:
        load.start()
    partners = [at(dz=d) for d in (4, -4)] + [at(dy=d) for d in Y_OFF[:0:-1]] + [at(dx=d) for d in (2, 1, 3)]
    partners += [at(dz=d) for d in (2, -2, 1, -1)] + [at(dc=1)]
    barrier = pltpu.get_barrier_semaphore()
    for p in partners:
        pl.semaphore_signal(barrier, inc=1, device_id=p, device_id_type=MESH)

    taken, unsent = [0], []

    def remote(k, src, dst, device):
        return pltpu.make_async_remote_copy(
            src_ref=src, dst_ref=dst, send_sem=send_sem.at[k], recv_sem=recv_sem.at[k],
            device_id=device, device_id_type=MESH,
        )

    def send_all(parts, whole):
        k = taken[0]
        taken[0] += 1
        for src, dst, device in parts:
            remote(k, src, dst, device).start()
        copy = remote(k, whole, whole, parts[0][2])
        unsent.append(copy)
        return copy

    def send(src, dst, device):
        return send_all([(src, dst, device)], dst)

    def wait_sent(n):
        for copy in unsent[:n]:
            copy.wait_send()
        del unsent[:n]

    def wait(*got):
        for copy in got:
            copy.wait_recv()

    def unit(ref):
        full = ref[...].astype(F32)
        inverse = lax.rsqrt(jnp.sum(full * full, axis=1, keepdims=True) + 1e-06)
        return full * inverse, inverse

    for load, ref, own in zip(loads, (img_ref, txt_ref), (lall.at[0, 0, 0], rall.at[0, 0, 0])):
        load.wait()
        own[...] = jnp.zeros((PAD, D), BF16)
        own[0:ROWS, :] = unit(ref)[0].astype(BF16)
    r = lax.broadcasted_iota(jnp.int32, sel.shape, 0)
    c = lax.broadcasted_iota(jnp.int32, sel.shape, 1)
    picked = ((c & 15) < ROWS) & ((c >> 4) * ROWS + (c & 15) == r)
    sel[...] = jnp.where(picked, 1.0, 0.0).astype(BF16)
    pl.semaphore_wait(barrier, len(partners))

    img_own, txt_own = lall.at[0, 0], rall.at[0, 0]
    main, rest = pl.ds(0, SPLIT), pl.ds(SPLIT, D - SPLIT)

    def y_first(*entries):
        to = [slot(Y_OFF, Y, -Y_OFF[j]) for j in entries]
        parts = [(txt_own.at[0, :, main], txt_own.at[t, :, main], at(dy=Y_OFF[j])) for t, j in zip(to, entries)]
        return send_all(parts, txt_own.at[pl.ds(min(entries), len(entries)), :, main])

    z_below = send(img_own.at[0], img_own.at[3], at(dz=4))
    z_above = send(img_own.at[0], img_own.at[2], at(dz=-4))
    x_rest = send_all(
        [(rall.at[0, 0, 0, :, rest], rall.at[0, X - d, 0, :, rest], at(dx=d)) for d in (2, 1, 3)],
        rall.at[0, pl.ds(1, NX - 1), 0, :, rest],
    )
    y_far = y_first(7, 5, 6)
    y_two, y_one = y_first(3, 4), y_first(1, 2)

    def x_send(lo, hi, straight=False):
        part = pl.ds(lo, hi - lo)
        got = {}
        if straight:
            got[2] = send(txt_own.at[part, :, main], rall.at[0, 2, part, :, main], at(dx=2))
        got[3] = send(txt_own.at[part, :, main], rall.at[0, 3, part, :, main], at(dx=1))
        got[1] = send(txt_own.at[part, :, main], rall.at[0, 1, part, :, main], at(dx=-1))
        return got

    def x_relay(got, frm, lo, hi):
        part = pl.ds(lo, hi - lo)
        wait(got[frm])
        to = at(dx=1 if frm == 3 else -1)
        got[2] = send(rall.at[0, frm, part, :, main], rall.at[0, 2, part, :, main], to)

    def n_send(lo, hi):
        part = pl.ds(lo, hi - lo)
        return {
            2: send(img_own.at[part], lall.at[0, 2, part], at(dz=1)),
            1: send(img_own.at[part], lall.at[0, 1, part], at(dz=-1)),
        }

    def n_relay(frm, entry):
        offset = Z_NEAR[frm] * 2 + Z_FAR[entry]
        to = slot(Z_LAST, Z, offset)
        return send(lall.at[0, frm, entry], lall.at[0, 3, to], at(dz=-Z_NEAR[frm]))

    n0 = n_send(0, 1)
    x0 = x_send(0, 1)
    wait(x_rest)
    near = [(j, slot(Y_OFF, Y, -Y_OFF[j])) for j in (7, 5, 6, 3, 4, 1, 2)]
    y_rest = send_all(
        [(rall.at[0, :, 0, :, rest], rall.at[0, :, t, :, rest], at(dy=Y_OFF[j])) for j, t in near],
        rall.at[0, :, pl.ds(1, NY - 1), :, rest],
    )
    wait(y_one)
    x1 = x_send(1, 3)
    x_relay(x0, 3, 0, 1)
    wait(y_two)
    x2 = x_send(3, 5)
    wait(z_below, z_above)
    low, high = pl.ds(0, 640), pl.ds(640, D - 640)
    z_eight = send_all(
        [
            (img_own.at[3, :, low], img_own.at[1, :, low], at(dz=4)),
            (img_own.at[2, :, high], img_own.at[1, :, high], at(dz=-4)),
        ],
        img_own.at[1],
    )
    n1 = n_send(2, 4)
    wait(n0[1], n0[2])
    last = [n_relay(1, 0), n_relay(2, 0)]
    wait(y_far)
    x3 = x_send(5, 8, straight=True)
    x_relay(x1, 1, 1, 3)
    x_relay(x2, 3, 3, 5)
    wait(n1[1], n1[2])
    last += [n_relay(1, 2), n_relay(2, 3)]
    wait(z_eight)
    n2 = n_send(1, 2)
    shared_l = [send(lall.at[0, 0], lall.at[1, 0], at(dc=1))]
    wait(x0[1], x1[3], x2[1])
    wait(y_rest)
    shared_r = [send(rall.at[0, 0], rall.at[1, 0], at(dc=1))]
    for s in (3, 1, 2):
        wait(x3[s])
        if s == 2:
            wait(x0[2], x1[2], x2[2])
        shared_r.append(send(rall.at[0, s], rall.at[1, s], at(dc=1)))
    for s in (2, 1):
        wait(n2[s])
        shared_l.append(send(lall.at[0, s], lall.at[1, s], at(dc=1)))
    wait(*last)
    shared_l.append(send(lall.at[0, 3], lall.at[1, 3], at(dc=1)))

    scale = jnp.exp(jnp.full((1, 1), ls_ref[0], F32))
    shift = jnp.full((1, 1), bias_ref[0], F32)
    dims = (((1,), (1,)), ((), ()))

    def sigmoid(logit):
        return 1.0 / (1.0 + jnp.exp(-logit))

    def row_blocks(core, ref, n):
        return ref.at[core].reshape(n, D)

    left = [row_blocks(i, lall, L_OWN) for i in range(2)]
    right = [row_blocks(i, rall, R_OWN) for i in range(2)]
    row_ok = (lax.broadcasted_iota(jnp.int32, (STEP, L_OWN), 0) & 15) < ROWS
    col_ok = (lax.broadcasted_iota(jnp.int32, (STEP, L_OWN), 1) & 15) < ROWS
    ok = jnp.where(row_ok & col_ok, 1.0, 0.0).astype(F32)

    def fold(a):
        return jnp.sum(a.reshape(STEP // 8, 8, a.shape[1]), axis=0)

    def text_weights(core, sums):
        cosb[:, 0:L_OWN] = lax.dot_general(right[0][...], left[core][...], dims, preferred_element_type=F32)
        cols = slice(core * L_OWN, (core + 1) * L_OWN)

        def weigh(i, sums):
            part = pl.ds(pl.multiple_of(i * STEP, STEP), STEP)
            cosine = cosb[part, 0:L_OWN]
            weight = sigmoid(scale * cosine + shift)
            wt[part, cols] = weight.astype(BF16)
            return sums[0] + fold(weight * cosine), sums[1] + fold(weight * ok)

        return lax.fori_loop(0, R_OWN // STEP, weigh, sums)

    def image_weights(core):
        cosb[0:L_OWN, :] = lax.dot_general(left[0][...], right[core][...], dims, preferred_element_type=F32)
        cols = slice(core * R_OWN, (core + 1) * R_OWN)

        def weigh(i, carry):
            part = pl.ds(pl.multiple_of(i * STEP, STEP), STEP)
            wb[part, cols] = sigmoid(scale * cosb[part, :] + shift).astype(BF16)
            return carry

        lax.fori_loop(0, L_OWN // STEP, weigh, 0)

    def lanes(a):
        return sum(a[:, 128 * i : 128 * (i + 1)] for i in range(a.shape[1] // 128))

    rows16 = lax.broadcasted_iota(jnp.int32, (PAD, 128), 0)
    cols16 = lax.broadcasted_iota(jnp.int32, (PAD, 128), 1)
    diagonal = rows16 == cols16
    counted = jnp.where(diagonal & (rows16 < ROWS), 1.0, 0.0).astype(F32)

    zero = jnp.zeros((8, L_OWN), F32)
    sums = text_weights(0, (zero, zero))
    cosine = cosb[0:PAD, 0:128]
    logit = scale * cosine + shift
    other, same = sigmoid(logit), -sigmoid(-logit)
    wt[0:PAD, 0:128] = jnp.where(diagonal, same, other).astype(BF16)
    change = (same - other) * counted
    change_scale = change * cosine
    wait(*shared_l)
    sums = text_weights(1, sums)
    stat[0, 0:8, :] = (lanes(sums[0]) + change_scale[0:8] + change_scale[8:16]) * scale
    stat[0, 8:16, :] = lanes(sums[1]) + change[0:8] + change[8:16]

    def stat_send(level, devices):
        parts = [(stat.at[level], stat_in.at[level, i], d) for i, d in enumerate(devices)]
        return send_all(parts, stat_in.at[level, pl.ds(0, len(parts))])

    def stat_take(level, got, n):
        wait(got)
        total = stat[level]
        for i in range(n):
            total += stat_in[level, i]
        stat[level + 1] = total

    stat_got = stat_send(0, [at(dz=4), at(dz=-4)])
    wtc[...] = jnp.dot(sel[...], wt[...], preferred_element_type=F32).astype(BF16)

    def cols_of(k):
        return pl.ds(k * WIDTH, WIDTH)

    x_in, z_in = {}, {}

    def text_part(k):
        t = jnp.dot(wtc[:, 0:L_OWN], left[0][:, cols_of(k)], preferred_element_type=F32)
        t += jnp.dot(wtc[:, L_OWN : 2 * L_OWN], left[1][:, cols_of(k)], preferred_element_type=F32)
        tp[k] = t.reshape(NX, XR, WIDTH)
        x_in[k] = [
            send(tp.at[k, 2, pl.ds(0, XR // 2)], tx1.at[k, 0], at(dx=1)),
            send(tp.at[k, 2, pl.ds(XR // 2, XR // 2)], tx1.at[k, 1], at(dx=-1)),
        ]

    def image_part(k):
        m = jnp.dot(wbc[:, 0:R_OWN], right[0][:, cols_of(k)], preferred_element_type=F32)
        m += jnp.dot(wbc[:, R_OWN : 2 * R_OWN], right[1][:, cols_of(k)], preferred_element_type=F32)
        ip[k] = m.reshape(NN, ZR, WIDTH)
        z_in[k] = [
            send(ip.at[k, 3, pl.ds(0, ZR // 2)], iz1.at[k, 0], at(dz=1)),
            send(ip.at[k, 3, pl.ds(ZR // 2, ZR // 2)], iz1.at[k, 1], at(dz=-1)),
        ]

    old = len(unsent)
    f_in, y_in = {}, {}

    def text_merge(k):
        wait(*x_in[k])
        tp[k, 1, 0 : XR // 2] += tx1[k, 0]
        tp[k, 3, XR // 2 : XR] += tx1[k, 1]
        x_in[k] = [send(tp.at[k, 1], tx2.at[k, 0], at(dx=1)), send(tp.at[k, 3], tx2.at[k, 1], at(dx=-1))]

    def image_merge(k):
        wait(*z_in[k])
        ip[k, 1, 0 : ZR // 2] += iz1[k, 0]
        ip[k, 2, 0 : ZR // 2] += iz1[k, 1]
        z_in[k] = [send(ip.at[k, 1], iz2.at[k, 0], at(dz=1)), send(ip.at[k, 2], iz2.at[k, 1], at(dz=-1))]

    for k in range(NC):
        text_part(k)
    image_weights(0)
    logit = scale * cosb[0:PAD, 0:128] + shift
    wb[0:PAD, 0:128] = jnp.where(diagonal, -sigmoid(-logit), sigmoid(logit)).astype(BF16)
    wait(*shared_r)
    image_weights(1)
    wbc[...] = jnp.dot(sel[0 : NN * ZR, 0:L_OWN], wb[...], preferred_element_type=F32).astype(BF16)
    for k in range(NC):
        image_part(k)
        text_merge(k)
        if k == 0:
            stat_take(0, stat_got, 2)
            stat_got = send(stat_in.at[0, 0], stat_in.at[1, 0], at(dz=4))
    wait_sent(old)
    for k in range(NC):
        image_merge(k)
    old = len(unsent)
    def far_send(k, entry):
        return send(ip.at[k, 0, window(entry)], iw.at[k, entry - 1], at(dz=Z_FAR[entry]))

    for k in range(NC):
        over, other = (2, 3) if k % 2 == 0 else (3, 2)
        wait(*z_in[k])
        ip[k, 0] += iz2[k, 0] + iz2[k, 1]
        f_in[k] = [
            send(ip.at[k, 0, window(1)], iw.at[k, 0], at(dz=Z_FAR[over])),
            far_send(k, other),
        ]
        wait(*x_in[k])
        tp[k, 0] += tx2[k, 0] + tx2[k, 1]
        y_in[k] = send_all(
            [(tp.at[k, 0, window(j)], ty.at[k, j - 1], at(dy=Y_OFF[j])) for j in (7, 5, 6, 3, 4, 1, 2)], ty.at[k]
        )
        if k == 0:
            stat_take(1, stat_got, 1)
            stat_got = stat_send(2, [at(dy=d) for d in Y_OFF[1:]])
    for k in range(NC):
        over = 2 if k % 2 == 0 else 3
        wait(f_in[k][0])
        if over % 2 == 0:
            fb[k, 0:ROWS] = ip[k, 0, 24:36] + iw[k, 0, PAD - ROWS : PAD]
        else:
            fb[k] = ip[k, 0, 32:48] + iw[k, 0]
        f_in[k][0] = send(fb.at[k], iw.at[k, over - 1], at(dz=Z_FAR[over]))
    stat_take(2, stat_got, NY - 1)
    stat_got = stat_send(3, [at(dx=d) for d in (1, 2, 3)])

    wait_sent(old)

    def total_of(own, ref, k, entries):
        even, odd = own, None
        for e in entries:
            got = ref[k, e - 1]
            if e % 2 == 0:
                even = even + got
            else:
                odd = got if odd is None else odd + got
        return even[0:ROWS] + odd[PAD - ROWS : PAD]

    def back(ref, total, out_ref):
        u, inverse = unit(ref)
        grad = scale * total
        out_ref[...] = (grad - u * jnp.sum(u * grad, axis=1, keepdims=True)) * inverse

    for k in range(NC):
        wait(*f_in[k])
    image_sums = [total_of(ip[k, 0, 0:PAD], iw, k, (2, 3)) for k in range(NC)]
    stat_take(3, stat_got, NX - 1)
    stat_got = stat_send(4, [at(dz=d) for d in (2, 1, -1)])
    back(img_ref, jnp.concatenate(image_sums, axis=1), ig_ref)
    for k in range(NC):
        wait(y_in[k])
    stat_take(4, stat_got, 3)
    stat_got = stat_send(5, [at(dc=1)])
    text_sums = [total_of(tp[k, 0, 0:PAD], ty, k, range(1, NY)) for k in range(NC)]
    back(txt_ref, jnp.concatenate(text_sums, axis=1), tg_ref)
    stat_take(5, stat_got, 1)
    st_ref[0] = jnp.sum(stat[6, 0:8, :])
    st_ref[1] = jnp.sum(stat[6, 8:16, :])
    wait_sent(len(unsent))


def shards(images, texts, log_scale, bias):
    vmem, smem = pl.BlockSpec(memory_space=pltpu.VMEM), pl.BlockSpec(memory_space=pltpu.SMEM)
    hbm = pl.BlockSpec(memory_space=pltpu.HBM)
    return pl.pallas_call(
        kernel,
        out_shape=(
            jax.ShapeDtypeStruct((ROWS, D), F32),
            jax.ShapeDtypeStruct((ROWS, D), F32),
            jax.ShapeDtypeStruct((2,), F32),
        ),
        in_specs=[hbm, hbm, smem, smem],
        out_specs=(vmem, vmem, smem),
        scratch_shapes=[
            pltpu.VMEM((ROWS, D), BF16),
            pltpu.VMEM((ROWS, D), BF16),
            pltpu.VMEM((2, NN, NF, PAD, D), BF16),
            pltpu.VMEM((2, NX, NY, PAD, D), BF16),
            pltpu.VMEM((R_OWN, R_OWN), F32),
            pltpu.VMEM((R_OWN, 2 * L_OWN), BF16),
            pltpu.VMEM((L_OWN, 2 * R_OWN), BF16),
            pltpu.VMEM((NX * XR, 2 * L_OWN), BF16),
            pltpu.VMEM((NN * ZR, 2 * R_OWN), BF16),
            pltpu.VMEM((NX * XR, R_OWN), BF16),
            pltpu.VMEM((NC, NX, XR, WIDTH), F32),
            pltpu.VMEM((NC, 2, XR // 2, WIDTH), F32),
            pltpu.VMEM((NC, 2, XR, WIDTH), F32),
            pltpu.VMEM((NC, NY - 1, PAD, WIDTH), F32),
            pltpu.VMEM((NC, NN, ZR, WIDTH), F32),
            pltpu.VMEM((NC, 2, ZR // 2, WIDTH), F32),
            pltpu.VMEM((NC, 2, ZR, WIDTH), F32),
            pltpu.VMEM((NC, NF - 1, PAD, WIDTH), F32),
            pltpu.VMEM((NC, PAD, WIDTH), F32),
            pltpu.VMEM((7, 16, 128), F32),
            pltpu.VMEM((6, NY - 1, 16, 128), F32),
            pltpu.SemaphoreType.DMA((2,)),
            pltpu.SemaphoreType.DMA((N_COPIES,)),
            pltpu.SemaphoreType.DMA((N_COPIES,)),
        ],
        compiler_params=pltpu.CompilerParams(
            collective_id=0, has_side_effects=True, vmem_limit_bytes=48 * 1024 * 1024
        ),
        cost_estimate=pl.CostEstimate(flops=3 * 2 * 512 * 512 * D, bytes_accessed=1 << 20, transcendentals=1 << 20),
        name="pair_gradients",
    )(images, texts, log_scale, bias)


def solution(mesh):
    rows = P(("dp", "group"), None)
    return jax.shard_map(
        shards, mesh=mesh, in_specs=(rows, rows, P(), P()), out_specs=(rows, rows, P()), check_vma=False
    )
```

```python
import jax
import jax.numpy as jnp
from jax import lax
from jax.experimental import pallas as pl
from jax.experimental.pallas import tpu as pltpu
from jax.sharding import PartitionSpec as P

D = 1152
ROWS = 12
PAD = 16
X, Y, Z = 4, 8, 16
Y_OFF = (0, 1, -1, 2, -2, 3, -3, 4)
Z_NEAR = (0, 1, -1)
Z_FAR = (0, 8, 4, -4)
Z_LAST = (2, -6, -2, 6)
NX, NY, NN, NF = 4, 8, 4, 4
L_OWN, R_OWN = NN * NF * PAD, NX * NY * PAD
XR, ZR = NY * ROWS, NF * ROWS
WIDTHS = (256, 512, 384)
BEGINS = (0, 256, 768)
NC = len(WIDTHS)
SPLIT = 896
MESH = pl.DeviceIdType.MESH
F32, BF16 = jnp.float32, jnp.bfloat16
STEP = 64
N_COPIES = 160


def slot(offsets, size, offset):
    return [o % size for o in offsets].index(offset % size)


def halves(width):
    first = 128 * ((width // 128 + 1) // 2)
    return first, width - first


def pack(dst, src, row):
    width = src.shape[1]
    first, second = halves(width)
    dst[:, 0:width] = src[row : row + 8, :]
    dst[0:4, width : width + first] = src[row + 8 : row + 12, 0:first]
    dst[4:8, width : width + second] = src[row + 8 : row + 12, first:width]
    if second < first:
        dst[4:8, width + second : width + first] = jnp.zeros((4, first - second), F32)


def unpack(dst, begin, got):
    width = [w for w, b in zip(WIDTHS, BEGINS) if b == begin][0]
    first, second = halves(width)
    dst[0:8, begin : begin + width] = got[:, 0:width]
    dst[8:12, begin : begin + first] = got[0:4, width : width + first]
    dst[8:12, begin + first : begin + width] = got[4:8, width : width + second]


def kernel(
    img_hbm, txt_hbm, ls_ref, bias_ref, ig_ref, tg_ref, st_ref,
    img_ref, txt_ref, lall, rall, cosb, wt, wb, wtc, wbc, sel, tp, tx1, tx2, ty, yb, ip, iz1, iz2, iw, zb, total,
    stat, stat_in, load_sem, send_sem, recv_sem,
):
    dp, group = lax.axis_index("dp"), lax.axis_index("group")
    zh, xx, yy = dp % 2, (dp // 2) % X, dp // (2 * X)
    zz, cc = zh * 8 + group // 2, group % 2

    def at(dx=0, dy=0, dz=0, dc=0):
        x, y, z, c = (xx + dx + X) % X, (yy + dy + Y) % Y, (zz + dz + Z) % Z, (cc + dc) % 2
        return ((y * X + x) * 2 + z // 8, (z % 8) * 2 + c)

    loads = [
        pltpu.make_async_copy(img_hbm, img_ref, load_sem.at[0]),
        pltpu.make_async_copy(txt_hbm, txt_ref, load_sem.at[1]),
    ]
    for load in loads:
        load.start()
    partners = [at(dz=d) for d in (4, -4)] + [at(dy=d) for d in Y_OFF[:0:-1]] + [at(dx=d) for d in (2, 1, 3)]
    partners += [at(dz=d) for d in (2, -2, 1, -1)] + [at(dc=1)]
    barrier = pltpu.get_barrier_semaphore()
    for p in partners:
        pl.semaphore_signal(barrier, inc=1, device_id=p, device_id_type=MESH)

    taken, unsent = [0], []

    def remote(k, src, dst, device):
        return pltpu.make_async_remote_copy(
            src_ref=src, dst_ref=dst, send_sem=send_sem.at[k], recv_sem=recv_sem.at[k],
            device_id=device, device_id_type=MESH,
        )

    def send_all(parts, whole):
        k = taken[0]
        taken[0] += 1
        for src, dst, device in parts:
            remote(k, src, dst, device).start()
        copy = remote(k, whole, whole, parts[0][2])
        unsent.append(copy)
        return copy

    def send(src, dst, device):
        return send_all([(src, dst, device)], dst)

    def wait_sent(n):
        for copy in unsent[:n]:
            copy.wait_send()
        del unsent[:n]

    def wait(*got):
        for copy in got:
            copy.wait_recv()

    def unit(ref):
        full = ref[...].astype(F32)
        inverse = lax.rsqrt(jnp.sum(full * full, axis=1, keepdims=True) + 1e-06)
        return full * inverse, inverse

    for load, ref, own in zip(loads, (img_ref, txt_ref), (lall.at[0, 0, 0], rall.at[0, 0, 0])):
        load.wait()
        own[...] = jnp.zeros((PAD, D), BF16)
        own[0:ROWS, :] = unit(ref)[0].astype(BF16)
    r = lax.broadcasted_iota(jnp.int32, sel.shape, 0)
    c = lax.broadcasted_iota(jnp.int32, sel.shape, 1)
    picked = ((c & 15) < ROWS) & ((c >> 4) * ROWS + (c & 15) == r)
    sel[...] = jnp.where(picked, 1.0, 0.0).astype(BF16)
    pl.semaphore_wait(barrier, len(partners))

    img_own, txt_own = lall.at[0, 0], rall.at[0, 0]
    main, rest = pl.ds(0, SPLIT), pl.ds(SPLIT, D - SPLIT)

    def y_first(*entries):
        to = [slot(Y_OFF, Y, -Y_OFF[j]) for j in entries]
        parts = [(txt_own.at[0, :, main], txt_own.at[t, :, main], at(dy=Y_OFF[j])) for t, j in zip(to, entries)]
        return send_all(parts, txt_own.at[pl.ds(min(entries), len(entries)), :, main])

    z_below = send(img_own.at[0], img_own.at[3], at(dz=4))
    z_above = send(img_own.at[0], img_own.at[2], at(dz=-4))
    x_rest = send_all(
        [(rall.at[0, 0, 0, :, rest], rall.at[0, X - d, 0, :, rest], at(dx=d)) for d in (2, 1, 3)],
        rall.at[0, pl.ds(1, NX - 1), 0, :, rest],
    )
    y_far = y_first(7, 5, 6)
    y_two, y_one = y_first(3, 4), y_first(1, 2)

    def x_send(lo, hi, straight=False):
        part = pl.ds(lo, hi - lo)
        got = {}
        if straight:
            got[2] = send(txt_own.at[part, :, main], rall.at[0, 2, part, :, main], at(dx=2))
        got[3] = send(txt_own.at[part, :, main], rall.at[0, 3, part, :, main], at(dx=1))
        got[1] = send(txt_own.at[part, :, main], rall.at[0, 1, part, :, main], at(dx=-1))
        return got

    def x_relay(got, frm, lo, hi):
        part = pl.ds(lo, hi - lo)
        wait(got[frm])
        to = at(dx=1 if frm == 3 else -1)
        got[2] = send(rall.at[0, frm, part, :, main], rall.at[0, 2, part, :, main], to)

    def n_send(lo, hi):
        part = pl.ds(lo, hi - lo)
        return {
            2: send(img_own.at[part], lall.at[0, 2, part], at(dz=1)),
            1: send(img_own.at[part], lall.at[0, 1, part], at(dz=-1)),
        }

    def n_relay(frm, entry):
        offset = Z_NEAR[frm] * 2 + Z_FAR[entry]
        to = slot(Z_LAST, Z, offset)
        return send(lall.at[0, frm, entry], lall.at[0, 3, to], at(dz=-Z_NEAR[frm]))

    n0 = n_send(0, 1)
    x0 = x_send(0, 1)
    wait(x_rest)
    near = [(j, slot(Y_OFF, Y, -Y_OFF[j])) for j in (7, 5, 6, 3, 4, 1, 2)]
    y_rest = send_all(
        [(rall.at[0, :, 0, :, rest], rall.at[0, :, t, :, rest], at(dy=Y_OFF[j])) for j, t in near],
        rall.at[0, :, pl.ds(1, NY - 1), :, rest],
    )
    wait(y_one)
    x1 = x_send(1, 3)
    x_relay(x0, 3, 0, 1)
    wait(y_two)
    x2 = x_send(3, 5)
    wait(z_below, z_above)
    low, high = pl.ds(0, 640), pl.ds(640, D - 640)
    z_eight = send_all(
        [
            (img_own.at[3, :, low], img_own.at[1, :, low], at(dz=4)),
            (img_own.at[2, :, high], img_own.at[1, :, high], at(dz=-4)),
        ],
        img_own.at[1],
    )
    n1 = n_send(2, 4)
    wait(n0[1], n0[2])
    last = [n_relay(1, 0), n_relay(2, 0)]
    wait(y_far)
    x3 = x_send(5, 8, straight=True)
    x_relay(x1, 1, 1, 3)
    x_relay(x2, 3, 3, 5)
    wait(n1[1], n1[2])
    last += [n_relay(1, 2), n_relay(2, 3)]
    wait(z_eight)
    n2 = n_send(1, 2)
    shared_l = [send(lall.at[0, 0], lall.at[1, 0], at(dc=1))]
    wait(x0[1], x1[3], x2[1])
    wait(y_rest)
    shared_r = [send(rall.at[0, 0], rall.at[1, 0], at(dc=1))]
    for s in (3, 1, 2):
        wait(x3[s])
        if s == 2:
            wait(x0[2], x1[2], x2[2])
        shared_r.append(send(rall.at[0, s], rall.at[1, s], at(dc=1)))
    for s in (2, 1):
        wait(n2[s])
        shared_l.append(send(lall.at[0, s], lall.at[1, s], at(dc=1)))
    wait(*last)
    shared_l.append(send(lall.at[0, 3], lall.at[1, 3], at(dc=1)))

    scale = jnp.exp(jnp.full((1, 1), ls_ref[0], F32))
    shift = jnp.full((1, 1), bias_ref[0], F32)
    dims = (((1,), (1,)), ((), ()))

    def sigmoid(logit):
        return 1.0 / (1.0 + jnp.exp(-logit))

    def row_blocks(core, ref, n):
        return ref.at[core].reshape(n, D)

    left = [row_blocks(i, lall, L_OWN) for i in range(2)]
    right = [row_blocks(i, rall, R_OWN) for i in range(2)]
    row_ok = (lax.broadcasted_iota(jnp.int32, (STEP, L_OWN), 0) & 15) < ROWS
    col_ok = (lax.broadcasted_iota(jnp.int32, (STEP, L_OWN), 1) & 15) < ROWS
    ok = jnp.where(row_ok & col_ok, 1.0, 0.0).astype(F32)

    def fold(a):
        return jnp.sum(a.reshape(STEP // 8, 8, a.shape[1]), axis=0)

    def text_weights(core, sums):
        cosb[:, 0:L_OWN] = lax.dot_general(right[0][...], left[core][...], dims, preferred_element_type=F32)
        cols = slice(core * L_OWN, (core + 1) * L_OWN)

        def weigh(i, sums):
            part = pl.ds(pl.multiple_of(i * STEP, STEP), STEP)
            cosine = cosb[part, 0:L_OWN]
            weight = sigmoid(scale * cosine + shift)
            wt[part, cols] = weight.astype(BF16)
            return sums[0] + fold(weight * cosine), sums[1] + fold(weight * ok)

        return lax.fori_loop(0, R_OWN // STEP, weigh, sums)

    def image_weights(core):
        cosb[0:L_OWN, :] = lax.dot_general(left[0][...], right[core][...], dims, preferred_element_type=F32)
        cols = slice(core * R_OWN, (core + 1) * R_OWN)

        def weigh(i, carry):
            part = pl.ds(pl.multiple_of(i * STEP, STEP), STEP)
            wb[part, cols] = sigmoid(scale * cosb[part, :] + shift).astype(BF16)
            return carry

        lax.fori_loop(0, L_OWN // STEP, weigh, 0)

    def lanes(a):
        return sum(a[:, 128 * i : 128 * (i + 1)] for i in range(a.shape[1] // 128))

    rows16 = lax.broadcasted_iota(jnp.int32, (PAD, 128), 0)
    cols16 = lax.broadcasted_iota(jnp.int32, (PAD, 128), 1)
    diagonal = rows16 == cols16
    counted = jnp.where(diagonal & (rows16 < ROWS), 1.0, 0.0).astype(F32)

    zero = jnp.zeros((8, L_OWN), F32)
    sums = text_weights(0, (zero, zero))
    cosine = cosb[0:PAD, 0:128]
    logit = scale * cosine + shift
    other, same = sigmoid(logit), -sigmoid(-logit)
    wt[0:PAD, 0:128] = jnp.where(diagonal, same, other).astype(BF16)
    change = (same - other) * counted
    change_scale = change * cosine
    wait(*shared_l)
    sums = text_weights(1, sums)
    stat[0, 0:8, :] = (lanes(sums[0]) + change_scale[0:8] + change_scale[8:16]) * scale
    stat[0, 8:16, :] = lanes(sums[1]) + change[0:8] + change[8:16]

    def stat_send(level, devices):
        parts = [(stat.at[level], stat_in.at[level, i], d) for i, d in enumerate(devices)]
        return send_all(parts, stat_in.at[level, pl.ds(0, len(parts))])

    def stat_take(level, got, n):
        wait(got)
        total = stat[level]
        for i in range(n):
            total += stat_in[level, i]
        stat[level + 1] = total

    stat_got = stat_send(0, [at(dz=4), at(dz=-4)])
    wtc[...] = jnp.dot(sel[...], wt[...], preferred_element_type=F32).astype(BF16)

    def cols_of(k):
        return pl.ds(BEGINS[k], WIDTHS[k])

    x_in, z_in = {}, {}

    def text_part(k):
        t = jnp.dot(wtc[:, 0:L_OWN], left[0][:, cols_of(k)], preferred_element_type=F32)
        t += jnp.dot(wtc[:, L_OWN : 2 * L_OWN], left[1][:, cols_of(k)], preferred_element_type=F32)
        tp[k][...] = t.reshape(NX, XR, WIDTHS[k])
        x_in[k] = [
            send(tp[k].at[2, pl.ds(0, XR // 2)], tx1[k].at[0], at(dx=1)),
            send(tp[k].at[2, pl.ds(XR // 2, XR // 2)], tx1[k].at[1], at(dx=-1)),
        ]

    def image_part(k):
        m = jnp.dot(wbc[:, 0:R_OWN], right[0][:, cols_of(k)], preferred_element_type=F32)
        m += jnp.dot(wbc[:, R_OWN : 2 * R_OWN], right[1][:, cols_of(k)], preferred_element_type=F32)
        ip[k][...] = m.reshape(NN, ZR, WIDTHS[k])
        z_in[k] = [
            send(ip[k].at[3, pl.ds(0, ZR // 2)], iz1[k].at[0], at(dz=1)),
            send(ip[k].at[3, pl.ds(ZR // 2, ZR // 2)], iz1[k].at[1], at(dz=-1)),
        ]

    old = len(unsent)
    f_in, y_in = {}, {}

    def text_merge(k):
        wait(*x_in[k])
        tp[k][1, 0 : XR // 2] += tx1[k][0]
        tp[k][3, XR // 2 : XR] += tx1[k][1]
        x_in[k] = [send(tp[k].at[1], tx2[k].at[0], at(dx=1)), send(tp[k].at[3], tx2[k].at[1], at(dx=-1))]

    def image_merge(k):
        wait(*z_in[k])
        ip[k][1, 0 : ZR // 2] += iz1[k][0]
        ip[k][2, 0 : ZR // 2] += iz1[k][1]
        z_in[k] = [send(ip[k].at[1], iz2[k].at[0], at(dz=1)), send(ip[k].at[2], iz2[k].at[1], at(dz=-1))]

    for k in range(NC):
        text_part(k)
    image_weights(0)
    logit = scale * cosb[0:PAD, 0:128] + shift
    wb[0:PAD, 0:128] = jnp.where(diagonal, -sigmoid(-logit), sigmoid(logit)).astype(BF16)
    wait(*shared_r)
    image_weights(1)
    wbc[...] = jnp.dot(sel[0 : NN * ZR, 0:L_OWN], wb[...], preferred_element_type=F32).astype(BF16)
    for k in range(NC):
        image_part(k)
        text_merge(k)
        if k == 0:
            stat_take(0, stat_got, 2)
            stat_got = send(stat_in.at[0, 0], stat_in.at[1, 0], at(dz=4))
    wait_sent(old)
    for k in range(NC):
        image_merge(k)
    old = len(unsent)
    for k in range(NC):
        over, other = (2, 3) if k % 2 == 0 else (3, 2)
        wait(*z_in[k])
        ip[k][0] += iz2[k][0] + iz2[k][1]
        for e in (1, 2, 3):
            pack(zb[k].at[e - 1], ip[k].at[0], ROWS * e)
        f_in[k] = [
            send(zb[k].at[0], iw[k].at[0], at(dz=Z_FAR[over])),
            send(zb[k].at[other - 1], iw[k].at[other - 1], at(dz=Z_FAR[other])),
        ]
        wait(*x_in[k])
        tp[k][0] += tx2[k][0] + tx2[k][1]
        for j in range(1, NY):
            pack(yb[k].at[j - 1], tp[k].at[0], ROWS * j)
        y_in[k] = send_all(
            [(yb[k].at[j - 1], ty[k].at[j - 1], at(dy=Y_OFF[j])) for j in (7, 5, 6, 3, 4, 1, 2)], ty[k]
        )
        if k == 0:
            stat_take(1, stat_got, 1)
            stat_got = stat_send(2, [at(dy=d) for d in Y_OFF[1:]])
    for k in range(NC):
        over = 2 if k % 2 == 0 else 3
        wait(f_in[k][0])
        zb[k][over - 1] += iw[k][0]
        f_in[k][0] = send(zb[k].at[over - 1], iw[k].at[over - 1], at(dz=Z_FAR[over]))
    stat_take(2, stat_got, NY - 1)
    stat_got = stat_send(3, [at(dx=d) for d in (1, 2, 3)])

    wait_sent(old)

    def total_of(i, own, got, entries):
        for k in range(NC):
            unpack(total.at[i], BEGINS[k], sum(got[k][e - 1] for e in entries))
        return total[i] + jnp.concatenate([own[k][0, 0:ROWS] for k in range(NC)], axis=1)

    def back(ref, total, out_ref):
        u, inverse = unit(ref)
        grad = scale * total
        out_ref[...] = (grad - u * jnp.sum(u * grad, axis=1, keepdims=True)) * inverse

    for k in range(NC):
        wait(*f_in[k])
    image_sums = total_of(0, ip, iw, (2, 3))
    stat_take(3, stat_got, NX - 1)
    stat_got = stat_send(4, [at(dz=d) for d in (2, 1, -1)])
    back(img_ref, image_sums, ig_ref)
    for k in range(NC):
        wait(y_in[k])
    stat_take(4, stat_got, 3)
    stat_got = stat_send(5, [at(dc=1)])
    back(txt_ref, total_of(1, tp, ty, range(1, NY)), tg_ref)
    stat_take(5, stat_got, 1)
    st_ref[0] = jnp.sum(stat[6, 0:8, :])
    st_ref[1] = jnp.sum(stat[6, 8:16, :])
    wait_sent(len(unsent))


def per_part(*dims):
    return tuple(pltpu.VMEM(dims + (w,), F32) for w in WIDTHS)


def packed(n):
    return tuple(pltpu.VMEM((n, 8, w + halves(w)[0]), F32) for w in WIDTHS)


def shards(images, texts, log_scale, bias):
    vmem, smem = pl.BlockSpec(memory_space=pltpu.VMEM), pl.BlockSpec(memory_space=pltpu.SMEM)
    hbm = pl.BlockSpec(memory_space=pltpu.HBM)
    return pl.pallas_call(
        kernel,
        out_shape=(
            jax.ShapeDtypeStruct((ROWS, D), F32),
            jax.ShapeDtypeStruct((ROWS, D), F32),
            jax.ShapeDtypeStruct((2,), F32),
        ),
        in_specs=[hbm, hbm, smem, smem],
        out_specs=(vmem, vmem, smem),
        scratch_shapes=[
            pltpu.VMEM((ROWS, D), BF16),
            pltpu.VMEM((ROWS, D), BF16),
            pltpu.VMEM((2, NN, NF, PAD, D), BF16),
            pltpu.VMEM((2, NX, NY, PAD, D), BF16),
            pltpu.VMEM((R_OWN, R_OWN), F32),
            pltpu.VMEM((R_OWN, 2 * L_OWN), BF16),
            pltpu.VMEM((L_OWN, 2 * R_OWN), BF16),
            pltpu.VMEM((NX * XR, 2 * L_OWN), BF16),
            pltpu.VMEM((NN * ZR, 2 * R_OWN), BF16),
            pltpu.VMEM((NX * XR, R_OWN), BF16),
            per_part(NX, XR),
            per_part(2, XR // 2),
            per_part(2, XR),
            packed(NY - 1),
            packed(NY - 1),
            per_part(NN, ZR),
            per_part(2, ZR // 2),
            per_part(2, ZR),
            packed(NF - 1),
            packed(NF - 1),
            pltpu.VMEM((2, ROWS, D), F32),
            pltpu.VMEM((7, 16, 128), F32),
            pltpu.VMEM((6, NY - 1, 16, 128), F32),
            pltpu.SemaphoreType.DMA((2,)),
            pltpu.SemaphoreType.DMA((N_COPIES,)),
            pltpu.SemaphoreType.DMA((N_COPIES,)),
        ],
        compiler_params=pltpu.CompilerParams(
            collective_id=0, has_side_effects=True, vmem_limit_bytes=48 * 1024 * 1024
        ),
        cost_estimate=pl.CostEstimate(flops=3 * 2 * 512 * 512 * D, bytes_accessed=1 << 20, transcendentals=1 << 20),
        name="pair_gradients",
    )(images, texts, log_scale, bias)


def solution(mesh):
    rows = P(("dp", "group"), None)
    return jax.shard_map(
        shards, mesh=mesh, in_specs=(rows, rows, P(), P()), out_specs=(rows, rows, P()), check_vma=False
    )
```

```python
import jax
import jax.numpy as jnp
from jax import lax
from jax.experimental import pallas as pl
from jax.experimental.pallas import tpu as pltpu
from jax.sharding import PartitionSpec as P

D = 1152
ROWS = 12
PAD = 16
X, Y, Z = 4, 8, 16
Y_OFF = (0, 1, -1, 2, -2, 3, -3, 4)
Z_NEAR = (0, 1, -1)
Z_FAR = (0, 8, 4, -4)
Z_LAST = (2, -6, -2, 6)
NX, NY, NN, NF = 4, 8, 4, 4
L_OWN, R_OWN = NN * NF * PAD, NX * NY * PAD
XR, ZR = NY * ROWS, NF * ROWS
WIDTHS = (512, 384, 256)
BEGINS = (0, 512, 896)
NC = len(WIDTHS)
SPLIT = 896
MESH = pl.DeviceIdType.MESH
F32, BF16 = jnp.float32, jnp.bfloat16
STEP = 64
N_COPIES = 160


def slot(offsets, size, offset):
    return [o % size for o in offsets].index(offset % size)


def halves(width):
    first = 128 * ((width // 128 + 1) // 2)
    return first, width - first


def pack(dst, src, row):
    width = src.shape[1]
    first, second = halves(width)
    dst[:, 0:width] = src[row : row + 8, :]
    dst[0:4, width : width + first] = src[row + 8 : row + 12, 0:first]
    dst[4:8, width : width + second] = src[row + 8 : row + 12, first:width]
    if second < first:
        dst[4:8, width + second : width + first] = jnp.zeros((4, first - second), F32)


def unpack(dst, begin, got):
    width = [w for w, b in zip(WIDTHS, BEGINS) if b == begin][0]
    first, second = halves(width)
    dst[0:8, begin : begin + width] = got[:, 0:width]
    dst[8:12, begin : begin + first] = got[0:4, width : width + first]
    dst[8:12, begin + first : begin + width] = got[4:8, width : width + second]


def kernel(
    img_hbm, txt_hbm, ls_ref, bias_ref, ig_ref, tg_ref, st_ref,
    img_ref, txt_ref, lall, rall, cosb, wt, wb, wtc, wbc, sel, tp, tx1, tx2, ty, yb, ip, iz1, iz2, iw, zb, total,
    stat, stat_in, load_sem, send_sem, recv_sem,
):
    dp, group = lax.axis_index("dp"), lax.axis_index("group")
    zh, xx, yy = dp % 2, (dp // 2) % X, dp // (2 * X)
    zz, cc = zh * 8 + group // 2, group % 2

    def at(dx=0, dy=0, dz=0, dc=0):
        x, y, z, c = (xx + dx + X) % X, (yy + dy + Y) % Y, (zz + dz + Z) % Z, (cc + dc) % 2
        return ((y * X + x) * 2 + z // 8, (z % 8) * 2 + c)

    loads = [
        pltpu.make_async_copy(img_hbm, img_ref, load_sem.at[0]),
        pltpu.make_async_copy(txt_hbm, txt_ref, load_sem.at[1]),
    ]
    for load in loads:
        load.start()
    partners = [at(dz=d) for d in (4, -4)] + [at(dy=d) for d in Y_OFF[:0:-1]] + [at(dx=d) for d in (2, 1, 3)]
    partners += [at(dz=d) for d in (2, -2, 1, -1)] + [at(dc=1)]
    barrier = pltpu.get_barrier_semaphore()
    for p in partners:
        pl.semaphore_signal(barrier, inc=1, device_id=p, device_id_type=MESH)

    taken, unsent = [0], []

    def remote(k, src, dst, device):
        return pltpu.make_async_remote_copy(
            src_ref=src, dst_ref=dst, send_sem=send_sem.at[k], recv_sem=recv_sem.at[k],
            device_id=device, device_id_type=MESH,
        )

    def send_all(parts, whole):
        k = taken[0]
        taken[0] += 1
        for src, dst, device in parts:
            remote(k, src, dst, device).start()
        copy = remote(k, whole, whole, parts[0][2])
        unsent.append(copy)
        return copy

    def send(src, dst, device):
        return send_all([(src, dst, device)], dst)

    def wait_sent(n):
        for copy in unsent[:n]:
            copy.wait_send()
        del unsent[:n]

    def wait(*got):
        for copy in got:
            copy.wait_recv()

    def unit(ref):
        full = ref[...].astype(F32)
        inverse = lax.rsqrt(jnp.sum(full * full, axis=1, keepdims=True) + 1e-06)
        return full * inverse, inverse

    for load, ref, own in zip(loads, (img_ref, txt_ref), (lall.at[0, 0, 0], rall.at[0, 0, 0])):
        load.wait()
        own[...] = jnp.zeros((PAD, D), BF16)
        own[0:ROWS, :] = unit(ref)[0].astype(BF16)
    r = lax.broadcasted_iota(jnp.int32, sel.shape, 0)
    c = lax.broadcasted_iota(jnp.int32, sel.shape, 1)
    picked = ((c & 15) < ROWS) & ((c >> 4) * ROWS + (c & 15) == r)
    sel[...] = jnp.where(picked, 1.0, 0.0).astype(BF16)
    pl.semaphore_wait(barrier, len(partners))

    img_own, txt_own = lall.at[0, 0], rall.at[0, 0]
    main, rest = pl.ds(0, SPLIT), pl.ds(SPLIT, D - SPLIT)

    def y_first(*entries):
        to = [slot(Y_OFF, Y, -Y_OFF[j]) for j in entries]
        parts = [(txt_own.at[0, :, main], txt_own.at[t, :, main], at(dy=Y_OFF[j])) for t, j in zip(to, entries)]
        return send_all(parts, txt_own.at[pl.ds(min(entries), len(entries)), :, main])

    z_below = send(img_own.at[0], img_own.at[3], at(dz=4))
    z_above = send(img_own.at[0], img_own.at[2], at(dz=-4))
    x_rest = send_all(
        [(rall.at[0, 0, 0, :, rest], rall.at[0, X - d, 0, :, rest], at(dx=d)) for d in (2, 1, 3)],
        rall.at[0, pl.ds(1, NX - 1), 0, :, rest],
    )
    y_far = y_first(7, 5, 6)
    y_two, y_one = y_first(3, 4), y_first(1, 2)

    def x_send(lo, hi, straight=False):
        part = pl.ds(lo, hi - lo)
        got = {}
        if straight:
            got[2] = send(txt_own.at[part, :, main], rall.at[0, 2, part, :, main], at(dx=2))
        got[3] = send(txt_own.at[part, :, main], rall.at[0, 3, part, :, main], at(dx=1))
        got[1] = send(txt_own.at[part, :, main], rall.at[0, 1, part, :, main], at(dx=-1))
        return got

    def x_relay(got, frm, lo, hi):
        part = pl.ds(lo, hi - lo)
        wait(got[frm])
        to = at(dx=1 if frm == 3 else -1)
        got[2] = send(rall.at[0, frm, part, :, main], rall.at[0, 2, part, :, main], to)

    def n_send(lo, hi):
        part = pl.ds(lo, hi - lo)
        return {
            2: send(img_own.at[part], lall.at[0, 2, part], at(dz=1)),
            1: send(img_own.at[part], lall.at[0, 1, part], at(dz=-1)),
        }

    def n_relay(frm, entry):
        offset = Z_NEAR[frm] * 2 + Z_FAR[entry]
        to = slot(Z_LAST, Z, offset)
        return send(lall.at[0, frm, entry], lall.at[0, 3, to], at(dz=-Z_NEAR[frm]))

    n0 = n_send(0, 1)
    x0 = x_send(0, 1)
    wait(x_rest)
    near = [(j, slot(Y_OFF, Y, -Y_OFF[j])) for j in (7, 5, 6, 3, 4, 1, 2)]
    y_rest = send_all(
        [(rall.at[0, :, 0, :, rest], rall.at[0, :, t, :, rest], at(dy=Y_OFF[j])) for j, t in near],
        rall.at[0, :, pl.ds(1, NY - 1), :, rest],
    )
    wait(y_one)
    x1 = x_send(1, 3)
    x_relay(x0, 3, 0, 1)
    wait(y_two)
    x2 = x_send(3, 5)
    wait(z_below, z_above)
    low, high = pl.ds(0, 640), pl.ds(640, D - 640)
    z_eight = send_all(
        [
            (img_own.at[3, :, low], img_own.at[1, :, low], at(dz=4)),
            (img_own.at[2, :, high], img_own.at[1, :, high], at(dz=-4)),
        ],
        img_own.at[1],
    )
    n1 = n_send(2, 4)
    wait(n0[1], n0[2])
    last = [n_relay(1, 0), n_relay(2, 0)]
    wait(y_far)
    x3 = x_send(5, 8, straight=True)
    x_relay(x1, 1, 1, 3)
    x_relay(x2, 3, 3, 5)
    wait(n1[1], n1[2])
    last += [n_relay(1, 2), n_relay(2, 3)]
    wait(z_eight)
    n2 = n_send(1, 2)
    shared_l = [send(lall.at[0, 0], lall.at[1, 0], at(dc=1))]
    wait(x0[1], x1[3], x2[1])
    wait(y_rest)
    shared_r = [send(rall.at[0, 0], rall.at[1, 0], at(dc=1))]
    for s in (3, 1, 2):
        wait(x3[s])
        if s == 2:
            wait(x0[2], x1[2], x2[2])
        shared_r.append(send(rall.at[0, s], rall.at[1, s], at(dc=1)))
    for s in (2, 1):
        wait(n2[s])
        shared_l.append(send(lall.at[0, s], lall.at[1, s], at(dc=1)))
    wait(*last)
    shared_l.append(send(lall.at[0, 3], lall.at[1, 3], at(dc=1)))

    scale = jnp.exp(jnp.full((1, 1), ls_ref[0], F32))
    shift = jnp.full((1, 1), bias_ref[0], F32)
    dims = (((1,), (1,)), ((), ()))

    def sigmoid(logit):
        return 1.0 / (1.0 + jnp.exp(-logit))

    def row_blocks(core, ref, n):
        return ref.at[core].reshape(n, D)

    left = [row_blocks(i, lall, L_OWN) for i in range(2)]
    right = [row_blocks(i, rall, R_OWN) for i in range(2)]
    row_ok = (lax.broadcasted_iota(jnp.int32, (STEP, L_OWN), 0) & 15) < ROWS
    col_ok = (lax.broadcasted_iota(jnp.int32, (STEP, L_OWN), 1) & 15) < ROWS
    ok = jnp.where(row_ok & col_ok, 1.0, 0.0).astype(F32)

    def fold(a):
        return jnp.sum(a.reshape(STEP // 8, 8, a.shape[1]), axis=0)

    def text_weights(core, sums):
        cosb[:, 0:L_OWN] = lax.dot_general(right[0][...], left[core][...], dims, preferred_element_type=F32)
        cols = slice(core * L_OWN, (core + 1) * L_OWN)

        def weigh(i, sums):
            part = pl.ds(pl.multiple_of(i * STEP, STEP), STEP)
            cosine = cosb[part, 0:L_OWN]
            weight = sigmoid(scale * cosine + shift)
            wt[part, cols] = weight.astype(BF16)
            return sums[0] + fold(weight * cosine), sums[1] + fold(weight * ok)

        return lax.fori_loop(0, R_OWN // STEP, weigh, sums)

    def image_weights(core):
        cosb[0:L_OWN, :] = lax.dot_general(left[0][...], right[core][...], dims, preferred_element_type=F32)
        cols = slice(core * R_OWN, (core + 1) * R_OWN)

        def weigh(i, carry):
            part = pl.ds(pl.multiple_of(i * STEP, STEP), STEP)
            wb[part, cols] = sigmoid(scale * cosb[part, :] + shift).astype(BF16)
            return carry

        lax.fori_loop(0, L_OWN // STEP, weigh, 0)

    def lanes(a):
        return sum(a[:, 128 * i : 128 * (i + 1)] for i in range(a.shape[1] // 128))

    rows16 = lax.broadcasted_iota(jnp.int32, (PAD, 128), 0)
    cols16 = lax.broadcasted_iota(jnp.int32, (PAD, 128), 1)
    diagonal = rows16 == cols16
    counted = jnp.where(diagonal & (rows16 < ROWS), 1.0, 0.0).astype(F32)

    zero = jnp.zeros((8, L_OWN), F32)
    sums = text_weights(0, (zero, zero))
    cosine = cosb[0:PAD, 0:128]
    logit = scale * cosine + shift
    other, same = sigmoid(logit), -sigmoid(-logit)
    wt[0:PAD, 0:128] = jnp.where(diagonal, same, other).astype(BF16)
    change = (same - other) * counted
    change_scale = change * cosine
    wait(*shared_l)
    sums = text_weights(1, sums)
    stat[0, 0:8, :] = (lanes(sums[0]) + change_scale[0:8] + change_scale[8:16]) * scale
    stat[0, 8:16, :] = lanes(sums[1]) + change[0:8] + change[8:16]

    def stat_send(level, devices):
        parts = [(stat.at[level], stat_in.at[level, i], d) for i, d in enumerate(devices)]
        return send_all(parts, stat_in.at[level, pl.ds(0, len(parts))])

    def stat_take(level, got, n):
        wait(got)
        total = stat[level]
        for i in range(n):
            total += stat_in[level, i]
        stat[level + 1] = total

    stat_got = stat_send(0, [at(dz=4), at(dz=-4)])
    wtc[...] = jnp.dot(sel[...], wt[...], preferred_element_type=F32).astype(BF16)

    def cols_of(k):
        return pl.ds(BEGINS[k], WIDTHS[k])

    x_in, z_in, x_out, z_out = {}, {}, {}, {}
    x_lo, x_hi = pl.ds(0, XR // 2), pl.ds(XR // 2, XR // 2)
    z_lo, z_hi = pl.ds(0, ZR // 2), pl.ds(ZR // 2, ZR // 2)

    def text_part(k):
        t = jnp.dot(wtc[:, 0:L_OWN], left[0][:, cols_of(k)], preferred_element_type=F32)
        t += jnp.dot(wtc[:, L_OWN : 2 * L_OWN], left[1][:, cols_of(k)], preferred_element_type=F32)
        tp[k][...] = t.reshape(NX, XR, WIDTHS[k])
        x_in[k] = [
            send(tp[k].at[2, x_lo], tx1[k].at[0], at(dx=1)),
            send(tp[k].at[2, x_hi], tx1[k].at[1], at(dx=-1)),
        ]
        x_out[k] = [
            send(tp[k].at[1, x_hi], tx2[k].at[0, x_hi], at(dx=1)),
            send(tp[k].at[3, x_lo], tx2[k].at[1, x_lo], at(dx=-1)),
        ]

    def image_part(k):
        m = jnp.dot(wbc[:, 0:R_OWN], right[0][:, cols_of(k)], preferred_element_type=F32)
        m += jnp.dot(wbc[:, R_OWN : 2 * R_OWN], right[1][:, cols_of(k)], preferred_element_type=F32)
        ip[k][...] = m.reshape(NN, ZR, WIDTHS[k])
        z_in[k] = [
            send(ip[k].at[3, z_lo], iz1[k].at[0], at(dz=1)),
            send(ip[k].at[3, z_hi], iz1[k].at[1], at(dz=-1)),
        ]
        z_out[k] = [
            send(ip[k].at[1, z_hi], iz2[k].at[0, z_hi], at(dz=1)),
            send(ip[k].at[2, z_hi], iz2[k].at[1, z_hi], at(dz=-1)),
        ]

    old = len(unsent)
    f_in, y_in = {}, {}

    def text_merge(k):
        wait(*x_in[k])
        tp[k][1, 0 : XR // 2] += tx1[k][0]
        tp[k][3, XR // 2 : XR] += tx1[k][1]
        x_out[k] += [
            send(tp[k].at[1, x_lo], tx2[k].at[0, x_lo], at(dx=1)),
            send(tp[k].at[3, x_hi], tx2[k].at[1, x_hi], at(dx=-1)),
        ]

    def image_merge(k):
        wait(*z_in[k])
        ip[k][1, 0 : ZR // 2] += iz1[k][0]
        ip[k][2, 0 : ZR // 2] += iz1[k][1]
        z_out[k] += [
            send(ip[k].at[1, z_lo], iz2[k].at[0, z_lo], at(dz=1)),
            send(ip[k].at[2, z_lo], iz2[k].at[1, z_lo], at(dz=-1)),
        ]

    for k in range(NC):
        text_part(k)
    image_weights(0)
    logit = scale * cosb[0:PAD, 0:128] + shift
    wb[0:PAD, 0:128] = jnp.where(diagonal, -sigmoid(-logit), sigmoid(logit)).astype(BF16)
    wait(*shared_r)
    image_weights(1)
    wbc[...] = jnp.dot(sel[0 : NN * ZR, 0:L_OWN], wb[...], preferred_element_type=F32).astype(BF16)
    image_part(0)
    text_merge(0)
    image_part(1)
    image_part(2)
    stat_take(0, stat_got, 2)
    stat_got = send(stat_in.at[0, 0], stat_in.at[1, 0], at(dz=4))
    image_merge(0)
    text_merge(1)
    image_merge(1)
    wait_sent(old)
    text_merge(2)
    image_merge(2)
    old = len(unsent)

    def image_far(k):
        over, other = (2, 3) if k % 2 == 0 else (3, 2)
        wait(*z_out[k])
        ip[k][0] += iz2[k][0] + iz2[k][1]
        for e in (1, 2, 3):
            pack(zb[k].at[e - 1], ip[k].at[0], ROWS * e)
        f_in[k] = [
            send(zb[k].at[0], iw[k].at[0], at(dz=Z_FAR[over])),
            send(zb[k].at[other - 1], iw[k].at[other - 1], at(dz=Z_FAR[other])),
        ]

    def image_over(k):
        over = 2 if k % 2 == 0 else 3
        wait(f_in[k][0])
        zb[k][over - 1] += iw[k][0]
        f_in[k][0] = send(zb[k].at[over - 1], iw[k].at[over - 1], at(dz=Z_FAR[over]))

    def text_far(k):
        wait(*x_out[k])
        tp[k][0] += tx2[k][0] + tx2[k][1]
        for j in range(1, NY):
            pack(yb[k].at[j - 1], tp[k].at[0], ROWS * j)
        y_in[k] = send_all(
            [(yb[k].at[j - 1], ty[k].at[j - 1], at(dy=Y_OFF[j])) for j in (7, 5, 6, 3, 4, 1, 2)], ty[k]
        )

    image_far(0)
    text_far(0)
    stat_take(1, stat_got, 1)
    stat_got = stat_send(2, [at(dy=d) for d in Y_OFF[1:]])
    image_far(1)
    image_far(2)
    text_far(1)
    image_over(0)
    image_over(1)
    text_far(2)
    image_over(2)
    stat_take(2, stat_got, NY - 1)
    stat_got = stat_send(3, [at(dx=d) for d in (1, 2, 3)])

    wait_sent(old)

    def total_of(i, own, got, entries):
        for k in range(NC):
            unpack(total.at[i], BEGINS[k], sum(got[k][e - 1] for e in entries))
        return total[i] + jnp.concatenate([own[k][0, 0:ROWS] for k in range(NC)], axis=1)

    def back(ref, total, out_ref):
        u, inverse = unit(ref)
        grad = scale * total
        out_ref[...] = (grad - u * jnp.sum(u * grad, axis=1, keepdims=True)) * inverse

    for k in range(NC):
        wait(*f_in[k])
    image_sums = total_of(0, ip, iw, (2, 3))
    stat_take(3, stat_got, NX - 1)
    stat_got = stat_send(4, [at(dz=d) for d in (2, 1, -1)])
    back(img_ref, image_sums, ig_ref)
    for k in range(NC):
        wait(y_in[k])
    stat_take(4, stat_got, 3)
    stat_got = stat_send(5, [at(dc=1)])
    back(txt_ref, total_of(1, tp, ty, range(1, NY)), tg_ref)
    stat_take(5, stat_got, 1)
    st_ref[0] = jnp.sum(stat[6, 0:8, :])
    st_ref[1] = jnp.sum(stat[6, 8:16, :])
    wait_sent(len(unsent))


def per_part(*dims):
    return tuple(pltpu.VMEM(dims + (w,), F32) for w in WIDTHS)


def packed(n):
    return tuple(pltpu.VMEM((n, 8, w + halves(w)[0]), F32) for w in WIDTHS)


def shards(images, texts, log_scale, bias):
    vmem, smem = pl.BlockSpec(memory_space=pltpu.VMEM), pl.BlockSpec(memory_space=pltpu.SMEM)
    hbm = pl.BlockSpec(memory_space=pltpu.HBM)
    return pl.pallas_call(
        kernel,
        out_shape=(
            jax.ShapeDtypeStruct((ROWS, D), F32),
            jax.ShapeDtypeStruct((ROWS, D), F32),
            jax.ShapeDtypeStruct((2,), F32),
        ),
        in_specs=[hbm, hbm, smem, smem],
        out_specs=(vmem, vmem, smem),
        scratch_shapes=[
            pltpu.VMEM((ROWS, D), BF16),
            pltpu.VMEM((ROWS, D), BF16),
            pltpu.VMEM((2, NN, NF, PAD, D), BF16),
            pltpu.VMEM((2, NX, NY, PAD, D), BF16),
            pltpu.VMEM((R_OWN, R_OWN), F32),
            pltpu.VMEM((R_OWN, 2 * L_OWN), BF16),
            pltpu.VMEM((L_OWN, 2 * R_OWN), BF16),
            pltpu.VMEM((NX * XR, 2 * L_OWN), BF16),
            pltpu.VMEM((NN * ZR, 2 * R_OWN), BF16),
            pltpu.VMEM((NX * XR, R_OWN), BF16),
            per_part(NX, XR),
            per_part(2, XR // 2),
            per_part(2, XR),
            packed(NY - 1),
            packed(NY - 1),
            per_part(NN, ZR),
            per_part(2, ZR // 2),
            per_part(2, ZR),
            packed(NF - 1),
            packed(NF - 1),
            pltpu.VMEM((2, ROWS, D), F32),
            pltpu.VMEM((7, 16, 128), F32),
            pltpu.VMEM((6, NY - 1, 16, 128), F32),
            pltpu.SemaphoreType.DMA((2,)),
            pltpu.SemaphoreType.DMA((N_COPIES,)),
            pltpu.SemaphoreType.DMA((N_COPIES,)),
        ],
        compiler_params=pltpu.CompilerParams(
            collective_id=0, has_side_effects=True, vmem_limit_bytes=48 * 1024 * 1024
        ),
        cost_estimate=pl.CostEstimate(flops=3 * 2 * 512 * 512 * D, bytes_accessed=1 << 20, transcendentals=1 << 20),
        name="pair_gradients",
    )(images, texts, log_scale, bias)


def solution(mesh):
    rows = P(("dp", "group"), None)
    return jax.shard_map(
        shards, mesh=mesh, in_specs=(rows, rows, P(), P()), out_specs=(rows, rows, P()), check_vma=False
    )
```

```python
import jax
import jax.numpy as jnp
from jax import lax
from jax.experimental import pallas as pl
from jax.experimental.pallas import tpu as pltpu
from jax.sharding import PartitionSpec as P

D = 1152
ROWS = 12
PAD = 16
X, Y, Z = 4, 8, 16
Y_OFF = (0, 1, -1, 2, -2, 3, -3, 4)
Z_NEAR = (0, 1, -1)
Z_FAR = (0, 8, 4, -4)
Z_LAST = (2, -6, -2, 6)
NX, NY, NN, NF = 4, 8, 4, 4
L_OWN, R_OWN = NN * NF * PAD, NX * NY * PAD
XR, ZR = NY * ROWS, NF * ROWS
WIDTHS = (512, 384, 256)
BEGINS = (0, 512, 896)
NC = len(WIDTHS)
SPLIT = 896
MESH = pl.DeviceIdType.MESH
F32, BF16 = jnp.float32, jnp.bfloat16
STEP = 64
N_COPIES = 160


def slot(offsets, size, offset):
    return [o % size for o in offsets].index(offset % size)


def halves(width):
    first = 128 * ((width // 128 + 1) // 2)
    return first, width - first


def pack(dst, src, row):
    width = src.shape[1]
    first, second = halves(width)
    dst[:, 0:width] = src[row : row + 8, :]
    dst[0:4, width : width + first] = src[row + 8 : row + 12, 0:first]
    dst[4:8, width : width + second] = src[row + 8 : row + 12, first:width]
    if second < first:
        dst[4:8, width + second : width + first] = jnp.zeros((4, first - second), F32)


def unpack(dst, begin, got):
    width = [w for w, b in zip(WIDTHS, BEGINS) if b == begin][0]
    first, second = halves(width)
    dst[0:8, begin : begin + width] = got[:, 0:width]
    dst[8:12, begin : begin + first] = got[0:4, width : width + first]
    dst[8:12, begin + first : begin + width] = got[4:8, width : width + second]


def kernel(
    img_hbm, txt_hbm, ls_ref, bias_ref, ig_ref, tg_ref, st_ref,
    img_ref, txt_ref, lall, rall, cosb, wt, wb, wtc, wbc, sel, tp, tx1, tx2, ty, yb, ip, iz1, iz2, iw, zb, total,
    stat, stat_in, load_sem, send_sem, recv_sem,
):
    dp, group = lax.axis_index("dp"), lax.axis_index("group")
    zh, xx, yy = dp % 2, (dp // 2) % X, dp // (2 * X)
    zz, cc = zh * 8 + group // 2, group % 2

    def at(dx=0, dy=0, dz=0, dc=0):
        x, y, z, c = (xx + dx + X) % X, (yy + dy + Y) % Y, (zz + dz + Z) % Z, (cc + dc) % 2
        return ((y * X + x) * 2 + z // 8, (z % 8) * 2 + c)

    loads = [
        pltpu.make_async_copy(img_hbm, img_ref, load_sem.at[0]),
        pltpu.make_async_copy(txt_hbm, txt_ref, load_sem.at[1]),
    ]
    for load in loads:
        load.start()
    partners = [at(dz=d) for d in (4, -4)] + [at(dy=d) for d in Y_OFF[:0:-1]] + [at(dx=d) for d in (2, 1, 3)]
    partners += [at(dz=d) for d in (2, -2, 1, -1)] + [at(dc=1)]
    barrier = pltpu.get_barrier_semaphore()
    for p in partners:
        pl.semaphore_signal(barrier, inc=1, device_id=p, device_id_type=MESH)

    taken, unsent = [0], []

    def remote(k, src, dst, device):
        return pltpu.make_async_remote_copy(
            src_ref=src, dst_ref=dst, send_sem=send_sem.at[k], recv_sem=recv_sem.at[k],
            device_id=device, device_id_type=MESH,
        )

    def send_all(parts, whole):
        k = taken[0]
        taken[0] += 1
        for src, dst, device in parts:
            remote(k, src, dst, device).start()
        copy = remote(k, whole, whole, parts[0][2])
        unsent.append(copy)
        return copy

    def send(src, dst, device):
        return send_all([(src, dst, device)], dst)

    def wait_sent(n):
        for copy in unsent[:n]:
            copy.wait_send()
        del unsent[:n]

    def wait(*got):
        for copy in got:
            copy.wait_recv()

    def unit(ref):
        full = ref[...].astype(F32)
        inverse = lax.rsqrt(jnp.sum(full * full, axis=1, keepdims=True) + 1e-06)
        return full * inverse, inverse

    for load, ref, own in zip(loads, (img_ref, txt_ref), (lall.at[0, 0, 0], rall.at[0, 0, 0])):
        load.wait()
        own[...] = jnp.zeros((PAD, D), BF16)
        own[0:ROWS, :] = unit(ref)[0].astype(BF16)
    r = lax.broadcasted_iota(jnp.int32, sel.shape, 0)
    c = lax.broadcasted_iota(jnp.int32, sel.shape, 1)
    picked = ((c & 15) < ROWS) & ((c >> 4) * ROWS + (c & 15) == r)
    sel[...] = jnp.where(picked, 1.0, 0.0).astype(BF16)
    pl.semaphore_wait(barrier, len(partners))

    img_own, txt_own = lall.at[0, 0], rall.at[0, 0]
    main, rest = pl.ds(0, SPLIT), pl.ds(SPLIT, D - SPLIT)

    def y_first(*entries):
        to = [slot(Y_OFF, Y, -Y_OFF[j]) for j in entries]
        parts = [(txt_own.at[0, :, main], txt_own.at[t, :, main], at(dy=Y_OFF[j])) for t, j in zip(to, entries)]
        return send_all(parts, txt_own.at[pl.ds(min(entries), len(entries)), :, main])

    z_below = send(img_own.at[0], img_own.at[3], at(dz=4))
    z_above = send(img_own.at[0], img_own.at[2], at(dz=-4))
    x_rest = send_all(
        [(rall.at[0, 0, 0, :, rest], rall.at[0, X - d, 0, :, rest], at(dx=d)) for d in (2, 1, 3)],
        rall.at[0, pl.ds(1, NX - 1), 0, :, rest],
    )
    y_far = y_first(7, 5, 6)
    y_two, y_one = y_first(3, 4), y_first(1, 2)

    def x_send(lo, hi, straight=False):
        part = pl.ds(lo, hi - lo)
        got = {}
        if straight:
            got[2] = send(txt_own.at[part, :, main], rall.at[0, 2, part, :, main], at(dx=2))
        got[3] = send(txt_own.at[part, :, main], rall.at[0, 3, part, :, main], at(dx=1))
        got[1] = send(txt_own.at[part, :, main], rall.at[0, 1, part, :, main], at(dx=-1))
        return got

    def x_relay(got, frm, lo, hi):
        part = pl.ds(lo, hi - lo)
        wait(got[frm])
        to = at(dx=1 if frm == 3 else -1)
        got[2] = send(rall.at[0, frm, part, :, main], rall.at[0, 2, part, :, main], to)

    def n_send(lo, hi):
        part = pl.ds(lo, hi - lo)
        return {
            2: send(img_own.at[part], lall.at[0, 2, part], at(dz=1)),
            1: send(img_own.at[part], lall.at[0, 1, part], at(dz=-1)),
        }

    def n_relay(frm, entry):
        offset = Z_NEAR[frm] * 2 + Z_FAR[entry]
        to = slot(Z_LAST, Z, offset)
        return send(lall.at[0, frm, entry], lall.at[0, 3, to], at(dz=-Z_NEAR[frm]))

    n0 = n_send(0, 1)
    x0 = x_send(0, 1)
    wait(x_rest)
    near = [(j, slot(Y_OFF, Y, -Y_OFF[j])) for j in (7, 5, 6, 3, 4, 1, 2)]
    y_rest = send_all(
        [(rall.at[0, :, 0, :, rest], rall.at[0, :, t, :, rest], at(dy=Y_OFF[j])) for j, t in near],
        rall.at[0, :, pl.ds(1, NY - 1), :, rest],
    )
    wait(y_one)
    x1 = x_send(1, 3)
    x_relay(x0, 3, 0, 1)
    wait(y_two)
    x2 = x_send(3, 5)
    wait(z_below, z_above)
    low, high = pl.ds(0, 640), pl.ds(640, D - 640)
    z_eight = send_all(
        [
            (img_own.at[3, :, low], img_own.at[1, :, low], at(dz=4)),
            (img_own.at[2, :, high], img_own.at[1, :, high], at(dz=-4)),
        ],
        img_own.at[1],
    )
    n1 = n_send(2, 4)
    wait(n0[1], n0[2])
    last = [n_relay(1, 0), n_relay(2, 0)]
    wait(y_far)
    x3 = x_send(5, 8, straight=True)
    x_relay(x1, 1, 1, 3)
    x_relay(x2, 3, 3, 5)
    wait(n1[1], n1[2])
    last += [n_relay(1, 2), n_relay(2, 3)]
    wait(z_eight)
    n2 = n_send(1, 2)
    shared_l = [send(lall.at[0, 0], lall.at[1, 0], at(dc=1))]
    wait(x0[1], x1[3], x2[1])
    wait(y_rest)
    shared_r = [send(rall.at[0, 0], rall.at[1, 0], at(dc=1))]
    for s in (3, 1, 2):
        wait(x3[s])
        if s == 2:
            wait(x0[2], x1[2], x2[2])
    far = pl.ds(1, NX - 1)
    shared_r.append(send(rall.at[0, far], rall.at[1, far], at(dc=1)))
    wait(n2[1], n2[2], *last)
    near = pl.ds(1, NN - 1)
    shared_l.append(send(lall.at[0, near], lall.at[1, near], at(dc=1)))

    scale = jnp.exp(jnp.full((1, 1), ls_ref[0], F32))
    shift = jnp.full((1, 1), bias_ref[0], F32)
    dims = (((1,), (1,)), ((), ()))

    def sigmoid(logit):
        return 1.0 / (1.0 + jnp.exp(-logit))

    def row_blocks(core, ref, n):
        return ref.at[core].reshape(n, D)

    left = [row_blocks(i, lall, L_OWN) for i in range(2)]
    right = [row_blocks(i, rall, R_OWN) for i in range(2)]
    row_ok = (lax.broadcasted_iota(jnp.int32, (STEP, L_OWN), 0) & 15) < ROWS
    col_ok = (lax.broadcasted_iota(jnp.int32, (STEP, L_OWN), 1) & 15) < ROWS
    ok = jnp.where(row_ok & col_ok, 1.0, 0.0).astype(F32)

    def fold(a):
        return jnp.sum(a.reshape(STEP // 8, 8, a.shape[1]), axis=0)

    def text_weights(core, sums):
        cosb[:, 0:L_OWN] = lax.dot_general(right[0][...], left[core][...], dims, preferred_element_type=F32)
        cols = slice(core * L_OWN, (core + 1) * L_OWN)

        def weigh(i, sums):
            part = pl.ds(pl.multiple_of(i * STEP, STEP), STEP)
            cosine = cosb[part, 0:L_OWN]
            weight = sigmoid(scale * cosine + shift)
            wt[part, cols] = weight.astype(BF16)
            return sums[0] + fold(weight * cosine), sums[1] + fold(weight * ok)

        return lax.fori_loop(0, R_OWN // STEP, weigh, sums)

    def image_weights(core):
        cosb[0:L_OWN, :] = lax.dot_general(left[0][...], right[core][...], dims, preferred_element_type=F32)
        cols = slice(core * R_OWN, (core + 1) * R_OWN)

        def weigh(i, carry):
            part = pl.ds(pl.multiple_of(i * STEP, STEP), STEP)
            wb[part, cols] = sigmoid(scale * cosb[part, :] + shift).astype(BF16)
            return carry

        lax.fori_loop(0, L_OWN // STEP, weigh, 0)

    def lanes(a):
        return sum(a[:, 128 * i : 128 * (i + 1)] for i in range(a.shape[1] // 128))

    rows16 = lax.broadcasted_iota(jnp.int32, (PAD, 128), 0)
    cols16 = lax.broadcasted_iota(jnp.int32, (PAD, 128), 1)
    diagonal = rows16 == cols16
    counted = jnp.where(diagonal & (rows16 < ROWS), 1.0, 0.0).astype(F32)

    zero = jnp.zeros((8, L_OWN), F32)
    sums = text_weights(0, (zero, zero))
    cosine = cosb[0:PAD, 0:128]
    logit = scale * cosine + shift
    other, same = sigmoid(logit), -sigmoid(-logit)
    wt[0:PAD, 0:128] = jnp.where(diagonal, same, other).astype(BF16)
    change = (same - other) * counted
    change_scale = change * cosine
    wait(*shared_l)
    sums = text_weights(1, sums)
    stat[0, 0:8, :] = (lanes(sums[0]) + change_scale[0:8] + change_scale[8:16]) * scale
    stat[0, 8:16, :] = lanes(sums[1]) + change[0:8] + change[8:16]

    def stat_send(level, devices):
        parts = [(stat.at[level], stat_in.at[level, i], d) for i, d in enumerate(devices)]
        return send_all(parts, stat_in.at[level, pl.ds(0, len(parts))])

    def stat_take(level, got, n):
        wait(got)
        total = stat[level]
        for i in range(n):
            total += stat_in[level, i]
        stat[level + 1] = total

    stat_got = stat_send(0, [at(dz=4), at(dz=-4)])
    wtc[...] = jnp.dot(sel[...], wt[...], preferred_element_type=F32).astype(BF16)

    def cols_of(k):
        return pl.ds(BEGINS[k], WIDTHS[k])

    x_in, z_in, x_out, z_out = {}, {}, {}, {}
    x_lo, x_hi = pl.ds(0, XR // 2), pl.ds(XR // 2, XR // 2)
    z_lo, z_hi = pl.ds(0, ZR // 2), pl.ds(ZR // 2, ZR // 2)

    def text_part(k):
        t = jnp.dot(wtc[:, 0:L_OWN], left[0][:, cols_of(k)], preferred_element_type=F32)
        t += jnp.dot(wtc[:, L_OWN : 2 * L_OWN], left[1][:, cols_of(k)], preferred_element_type=F32)
        tp[k][...] = t.reshape(NX, XR, WIDTHS[k])
        x_in[k] = [
            send(tp[k].at[2, x_lo], tx1[k].at[0], at(dx=1)),
            send(tp[k].at[2, x_hi], tx1[k].at[1], at(dx=-1)),
        ]

    def image_part(k):
        m = jnp.dot(wbc[:, 0:R_OWN], right[0][:, cols_of(k)], preferred_element_type=F32)
        m += jnp.dot(wbc[:, R_OWN : 2 * R_OWN], right[1][:, cols_of(k)], preferred_element_type=F32)
        ip[k][...] = m.reshape(NN, ZR, WIDTHS[k])
        z_in[k] = [
            send(ip[k].at[3, z_lo], iz1[k].at[0], at(dz=1)),
            send(ip[k].at[3, z_hi], iz1[k].at[1], at(dz=-1)),
        ]

    old = len(unsent)
    f_in, y_in = {}, {}

    def text_merge(k):
        wait(*x_in[k])
        tp[k][1, 0 : XR // 2] += tx1[k][0]
        tp[k][3, XR // 2 : XR] += tx1[k][1]
        x_out[k] = [send(tp[k].at[1], tx2[k].at[0], at(dx=1)), send(tp[k].at[3], tx2[k].at[1], at(dx=-1))]

    def image_merge(k):
        wait(*z_in[k])
        ip[k][1, 0 : ZR // 2] += iz1[k][0]
        ip[k][2, 0 : ZR // 2] += iz1[k][1]
        z_out[k] = [send(ip[k].at[1], iz2[k].at[0], at(dz=1)), send(ip[k].at[2], iz2[k].at[1], at(dz=-1))]

    for k in range(NC):
        text_part(k)
    image_weights(0)
    logit = scale * cosb[0:PAD, 0:128] + shift
    wb[0:PAD, 0:128] = jnp.where(diagonal, -sigmoid(-logit), sigmoid(logit)).astype(BF16)
    wait(*shared_r)
    image_weights(1)
    wbc[...] = jnp.dot(sel[0 : NN * ZR, 0:L_OWN], wb[...], preferred_element_type=F32).astype(BF16)
    image_part(0)
    text_merge(0)
    image_part(1)
    image_part(2)
    stat_take(0, stat_got, 2)
    stat_got = send(stat_in.at[0, 0], stat_in.at[1, 0], at(dz=4))
    image_merge(0)
    text_merge(1)
    image_merge(1)
    wait_sent(old)
    text_merge(2)
    image_merge(2)
    old = len(unsent)

    def image_far(k):
        over, other = (2, 3) if k % 2 == 0 else (3, 2)
        wait(*z_out[k])
        ip[k][0] += iz2[k][0] + iz2[k][1]
        for e in (1, 2, 3):
            pack(zb[k].at[e - 1], ip[k].at[0], ROWS * e)
        f_in[k] = [
            send(zb[k].at[0], iw[k].at[0], at(dz=Z_FAR[over])),
            send(zb[k].at[other - 1], iw[k].at[other - 1], at(dz=Z_FAR[other])),
        ]

    def image_over(k):
        over = 2 if k % 2 == 0 else 3
        wait(f_in[k][0])
        zb[k][over - 1] += iw[k][0]
        f_in[k][0] = send(zb[k].at[over - 1], iw[k].at[over - 1], at(dz=Z_FAR[over]))

    def text_far(k):
        wait(*x_out[k])
        tp[k][0] += tx2[k][0] + tx2[k][1]
        for j in range(1, NY):
            pack(yb[k].at[j - 1], tp[k].at[0], ROWS * j)
        y_in[k] = send_all(
            [(yb[k].at[j - 1], ty[k].at[j - 1], at(dy=Y_OFF[j])) for j in (7, 5, 6, 3, 4, 1, 2)], ty[k]
        )

    image_far(0)
    text_far(0)
    stat_take(1, stat_got, 1)
    stat_got = stat_send(2, [at(dy=d) for d in Y_OFF[1:]])
    image_far(1)
    image_far(2)
    text_far(1)
    image_over(0)
    image_over(1)
    text_far(2)
    image_over(2)
    stat_take(2, stat_got, NY - 1)
    stat_got = stat_send(3, [at(dx=d) for d in (1, 2, 3)])

    wait_sent(old)

    def total_of(i, own, got, entries):
        for k in range(NC):
            unpack(total.at[i], BEGINS[k], sum(got[k][e - 1] for e in entries))
        return total[i] + jnp.concatenate([own[k][0, 0:ROWS] for k in range(NC)], axis=1)

    def back(ref, total, out_ref):
        u, inverse = unit(ref)
        grad = scale * total
        out_ref[...] = (grad - u * jnp.sum(u * grad, axis=1, keepdims=True)) * inverse

    for k in range(NC):
        wait(*f_in[k])
    image_sums = total_of(0, ip, iw, (2, 3))
    stat_take(3, stat_got, NX - 1)
    stat_got = stat_send(4, [at(dz=d) for d in (2, 1, -1)])
    back(img_ref, image_sums, ig_ref)
    for k in range(NC):
        wait(y_in[k])
    stat_take(4, stat_got, 3)
    stat_got = stat_send(5, [at(dc=1)])
    back(txt_ref, total_of(1, tp, ty, range(1, NY)), tg_ref)
    stat_take(5, stat_got, 1)
    st_ref[0] = jnp.sum(stat[6, 0:8, :])
    st_ref[1] = jnp.sum(stat[6, 8:16, :])
    wait_sent(len(unsent))


def per_part(*dims):
    return tuple(pltpu.VMEM(dims + (w,), F32) for w in WIDTHS)


def packed(n):
    return tuple(pltpu.VMEM((n, 8, w + halves(w)[0]), F32) for w in WIDTHS)


def shards(images, texts, log_scale, bias):
    vmem, smem = pl.BlockSpec(memory_space=pltpu.VMEM), pl.BlockSpec(memory_space=pltpu.SMEM)
    hbm = pl.BlockSpec(memory_space=pltpu.HBM)
    return pl.pallas_call(
        kernel,
        out_shape=(
            jax.ShapeDtypeStruct((ROWS, D), F32),
            jax.ShapeDtypeStruct((ROWS, D), F32),
            jax.ShapeDtypeStruct((2,), F32),
        ),
        in_specs=[hbm, hbm, smem, smem],
        out_specs=(vmem, vmem, smem),
        scratch_shapes=[
            pltpu.VMEM((ROWS, D), BF16),
            pltpu.VMEM((ROWS, D), BF16),
            pltpu.VMEM((2, NN, NF, PAD, D), BF16),
            pltpu.VMEM((2, NX, NY, PAD, D), BF16),
            pltpu.VMEM((R_OWN, R_OWN), F32),
            pltpu.VMEM((R_OWN, 2 * L_OWN), BF16),
            pltpu.VMEM((L_OWN, 2 * R_OWN), BF16),
            pltpu.VMEM((NX * XR, 2 * L_OWN), BF16),
            pltpu.VMEM((NN * ZR, 2 * R_OWN), BF16),
            pltpu.VMEM((NX * XR, R_OWN), BF16),
            per_part(NX, XR),
            per_part(2, XR // 2),
            per_part(2, XR),
            packed(NY - 1),
            packed(NY - 1),
            per_part(NN, ZR),
            per_part(2, ZR // 2),
            per_part(2, ZR),
            packed(NF - 1),
            packed(NF - 1),
            pltpu.VMEM((2, ROWS, D), F32),
            pltpu.VMEM((7, 16, 128), F32),
            pltpu.VMEM((6, NY - 1, 16, 128), F32),
            pltpu.SemaphoreType.DMA((2,)),
            pltpu.SemaphoreType.DMA((N_COPIES,)),
            pltpu.SemaphoreType.DMA((N_COPIES,)),
        ],
        compiler_params=pltpu.CompilerParams(
            collective_id=0, has_side_effects=True, vmem_limit_bytes=48 * 1024 * 1024
        ),
        cost_estimate=pl.CostEstimate(flops=3 * 2 * 512 * 512 * D, bytes_accessed=1 << 20, transcendentals=1 << 20),
        name="pair_gradients",
    )(images, texts, log_scale, bias)


def solution(mesh):
    rows = P(("dp", "group"), None)
    return jax.shard_map(
        shards, mesh=mesh, in_specs=(rows, rows, P(), P()), out_specs=(rows, rows, P()), check_vma=False
    )
```

```python
import jax
import jax.numpy as jnp
from jax import lax
from jax.experimental import pallas as pl
from jax.experimental.pallas import tpu as pltpu
from jax.sharding import PartitionSpec as P

D = 1152
ROWS = 12
PAD = 16
X, Y, Z = 4, 8, 16
Y_OFF = (0, 1, -1, 2, -2, 3, -3, 4)
Z_NEAR = (0, 1, -1)
Z_FAR = (0, 8, 4, -4)
Z_LAST = (2, -6, -2, 6)
NX, NY, NN, NF = 4, 8, 4, 4
L_OWN, R_OWN = NN * NF * PAD, NX * NY * PAD
XR, ZR = NY * ROWS, NF * ROWS
WIDTHS = (512, 384, 256)
BEGINS = (0, 512, 896)
NC = len(WIDTHS)
SPLIT = 896
MESH = pl.DeviceIdType.MESH
F32, BF16 = jnp.float32, jnp.bfloat16
STEP = 64
N_COPIES = 160


def slot(offsets, size, offset):
    return [o % size for o in offsets].index(offset % size)


def halves(width):
    first = 128 * ((width // 128 + 1) // 2)
    return first, width - first


def pack(dst, src, row):
    width = src.shape[1]
    first, second = halves(width)
    dst[:, 0:width] = src[row : row + 8, :]
    dst[0:4, width : width + first] = src[row + 8 : row + 12, 0:first]
    dst[4:8, width : width + second] = src[row + 8 : row + 12, first:width]
    if second < first:
        dst[4:8, width + second : width + first] = jnp.zeros((4, first - second), F32)


def unpack(dst, begin, got):
    width = [w for w, b in zip(WIDTHS, BEGINS) if b == begin][0]
    first, second = halves(width)
    dst[0:8, begin : begin + width] = got[:, 0:width]
    dst[8:12, begin : begin + first] = got[0:4, width : width + first]
    dst[8:12, begin + first : begin + width] = got[4:8, width : width + second]


def kernel(
    img_hbm, txt_hbm, ls_ref, bias_ref, ig_ref, tg_ref, st_ref,
    img_ref, txt_ref, lall, rall, cosb, wt, wb, wtc, wbc, sel, tp, tx1, tx2, ty, yb, ip, iz1, iz2, iw, zb, total,
    stat, stat_in, load_sem, send_sem, recv_sem,
):
    dp, group = lax.axis_index("dp"), lax.axis_index("group")
    zh, xx, yy = dp % 2, (dp // 2) % X, dp // (2 * X)
    zz, cc = zh * 8 + group // 2, group % 2

    def at(dx=0, dy=0, dz=0, dc=0):
        x, y, z, c = (xx + dx + X) % X, (yy + dy + Y) % Y, (zz + dz + Z) % Z, (cc + dc) % 2
        return ((y * X + x) * 2 + z // 8, (z % 8) * 2 + c)

    loads = [
        pltpu.make_async_copy(img_hbm, img_ref, load_sem.at[0]),
        pltpu.make_async_copy(txt_hbm, txt_ref, load_sem.at[1]),
    ]
    for load in loads:
        load.start()
    partners = [at(dz=d) for d in (4, -4)] + [at(dy=d) for d in Y_OFF[:0:-1]] + [at(dx=d) for d in (2, 1, 3)]
    partners += [at(dz=d) for d in (2, -2, 1, -1)] + [at(dc=1)]
    barrier = pltpu.get_barrier_semaphore()
    for p in partners:
        pl.semaphore_signal(barrier, inc=1, device_id=p, device_id_type=MESH)

    taken, unsent = [0], []

    def remote(k, src, dst, device):
        return pltpu.make_async_remote_copy(
            src_ref=src, dst_ref=dst, send_sem=send_sem.at[k], recv_sem=recv_sem.at[k],
            device_id=device, device_id_type=MESH,
        )

    def send_all(parts, whole):
        k = taken[0]
        taken[0] += 1
        for src, dst, device in parts:
            remote(k, src, dst, device).start()
        copy = remote(k, whole, whole, parts[0][2])
        unsent.append(copy)
        return copy

    def send(src, dst, device):
        return send_all([(src, dst, device)], dst)

    def wait_sent(n):
        for copy in unsent[:n]:
            copy.wait_send()
        del unsent[:n]

    def wait(*got):
        for copy in got:
            copy.wait_recv()

    def unit(ref):
        full = ref[...].astype(F32)
        inverse = lax.rsqrt(jnp.sum(full * full, axis=1, keepdims=True) + 1e-06)
        return full * inverse, inverse

    for load, ref, own in zip(loads, (img_ref, txt_ref), (lall.at[0, 0, 0], rall.at[0, 0, 0])):
        load.wait()
        own[...] = jnp.zeros((PAD, D), BF16)
        own[0:ROWS, :] = unit(ref)[0].astype(BF16)
    r = lax.broadcasted_iota(jnp.int32, sel.shape, 0)
    c = lax.broadcasted_iota(jnp.int32, sel.shape, 1)
    picked = ((c & 15) < ROWS) & ((c >> 4) * ROWS + (c & 15) == r)
    sel[...] = jnp.where(picked, 1.0, 0.0).astype(BF16)
    pl.semaphore_wait(barrier, len(partners))

    img_own, txt_own = lall.at[0, 0], rall.at[0, 0]
    main, rest = pl.ds(0, SPLIT), pl.ds(SPLIT, D - SPLIT)

    def y_first(*entries):
        to = [slot(Y_OFF, Y, -Y_OFF[j]) for j in entries]
        parts = [(txt_own.at[0, :, main], txt_own.at[t, :, main], at(dy=Y_OFF[j])) for t, j in zip(to, entries)]
        return send_all(parts, txt_own.at[pl.ds(min(entries), len(entries)), :, main])

    z_below = send(img_own.at[0], img_own.at[3], at(dz=4))
    z_above = send(img_own.at[0], img_own.at[2], at(dz=-4))
    x_own = send_all(
        [(txt_own.at[0], rall.at[0, X - d, 0], at(dx=d)) for d in (2, 1, 3)],
        rall.at[0, pl.ds(1, NX - 1), 0],
    )
    y_far = y_first(7, 5, 6)
    y_two, y_one = y_first(3, 4), y_first(1, 2)

    def x_send(lo, hi, straight=False):
        part = pl.ds(lo, hi - lo)
        got = {}
        if straight:
            got[2] = send(txt_own.at[part, :, main], rall.at[0, 2, part, :, main], at(dx=2))
        got[3] = send(txt_own.at[part, :, main], rall.at[0, 3, part, :, main], at(dx=1))
        got[1] = send(txt_own.at[part, :, main], rall.at[0, 1, part, :, main], at(dx=-1))
        return got

    def x_relay(got, frm, lo, hi):
        part = pl.ds(lo, hi - lo)
        wait(got[frm])
        to = at(dx=1 if frm == 3 else -1)
        got[2] = send(rall.at[0, frm, part, :, main], rall.at[0, 2, part, :, main], to)

    def n_send(lo, hi):
        part = pl.ds(lo, hi - lo)
        return {
            2: send(img_own.at[part], lall.at[0, 2, part], at(dz=1)),
            1: send(img_own.at[part], lall.at[0, 1, part], at(dz=-1)),
        }

    def n_relay(frm, entry):
        offset = Z_NEAR[frm] * 2 + Z_FAR[entry]
        to = slot(Z_LAST, Z, offset)
        return send(lall.at[0, frm, entry], lall.at[0, 3, to], at(dz=-Z_NEAR[frm]))

    n0 = n_send(0, 1)
    wait(x_own)
    near = [(j, slot(Y_OFF, Y, -Y_OFF[j])) for j in (7, 5, 6, 3, 4, 1, 2)]
    y_rest = send_all(
        [(rall.at[0, :, 0, :, rest], rall.at[0, :, t, :, rest], at(dy=Y_OFF[j])) for j, t in near],
        rall.at[0, :, pl.ds(1, NY - 1), :, rest],
    )
    wait(y_one)
    x1 = x_send(1, 3)
    wait(y_two)
    x2 = x_send(3, 5)
    wait(z_below, z_above)
    low, high = pl.ds(0, 640), pl.ds(640, D - 640)
    z_eight = send_all(
        [
            (img_own.at[3, :, low], img_own.at[1, :, low], at(dz=4)),
            (img_own.at[2, :, high], img_own.at[1, :, high], at(dz=-4)),
        ],
        img_own.at[1],
    )
    n1 = n_send(2, 4)
    wait(n0[1], n0[2])
    last = [n_relay(1, 0), n_relay(2, 0)]
    wait(y_far)
    x3 = x_send(5, 8, straight=True)
    x_relay(x1, 1, 1, 3)
    x_relay(x2, 3, 3, 5)
    wait(n1[1], n1[2])
    last += [n_relay(1, 2), n_relay(2, 3)]
    wait(z_eight)
    n2 = n_send(1, 2)
    shared_l = [send(lall.at[0, 0], lall.at[1, 0], at(dc=1))]
    wait(x1[3], x2[1])
    wait(y_rest)
    shared_r = [send(rall.at[0, 0], rall.at[1, 0], at(dc=1))]
    for s in (3, 1, 2):
        wait(x3[s])
        if s == 2:
            wait(x1[2], x2[2])
    far = pl.ds(1, NX - 1)
    shared_r.append(send(rall.at[0, far], rall.at[1, far], at(dc=1)))
    wait(n2[1], n2[2], *last)
    near = pl.ds(1, NN - 1)
    shared_l.append(send(lall.at[0, near], lall.at[1, near], at(dc=1)))

    scale = jnp.exp(jnp.full((1, 1), ls_ref[0], F32))
    shift = jnp.full((1, 1), bias_ref[0], F32)
    dims = (((1,), (1,)), ((), ()))

    def sigmoid(logit):
        return 1.0 / (1.0 + jnp.exp(-logit))

    def row_blocks(core, ref, n):
        return ref.at[core].reshape(n, D)

    left = [row_blocks(i, lall, L_OWN) for i in range(2)]
    right = [row_blocks(i, rall, R_OWN) for i in range(2)]
    row_ok = (lax.broadcasted_iota(jnp.int32, (STEP, L_OWN), 0) & 15) < ROWS
    col_ok = (lax.broadcasted_iota(jnp.int32, (STEP, L_OWN), 1) & 15) < ROWS
    ok = jnp.where(row_ok & col_ok, 1.0, 0.0).astype(F32)

    def fold(a):
        return jnp.sum(a.reshape(STEP // 8, 8, a.shape[1]), axis=0)

    def text_weights(core, sums):
        cosb[:, 0:L_OWN] = lax.dot_general(right[0][...], left[core][...], dims, preferred_element_type=F32)
        cols = slice(core * L_OWN, (core + 1) * L_OWN)

        def weigh(i, sums):
            part = pl.ds(pl.multiple_of(i * STEP, STEP), STEP)
            cosine = cosb[part, 0:L_OWN]
            weight = sigmoid(scale * cosine + shift)
            wt[part, cols] = weight.astype(BF16)
            return sums[0] + fold(weight * cosine), sums[1] + fold(weight * ok)

        return lax.fori_loop(0, R_OWN // STEP, weigh, sums)

    def image_weights(core):
        cosb[0:L_OWN, :] = lax.dot_general(left[0][...], right[core][...], dims, preferred_element_type=F32)
        cols = slice(core * R_OWN, (core + 1) * R_OWN)

        def weigh(i, carry):
            part = pl.ds(pl.multiple_of(i * STEP, STEP), STEP)
            wb[part, cols] = sigmoid(scale * cosb[part, :] + shift).astype(BF16)
            return carry

        lax.fori_loop(0, L_OWN // STEP, weigh, 0)

    def lanes(a):
        return sum(a[:, 128 * i : 128 * (i + 1)] for i in range(a.shape[1] // 128))

    rows16 = lax.broadcasted_iota(jnp.int32, (PAD, 128), 0)
    cols16 = lax.broadcasted_iota(jnp.int32, (PAD, 128), 1)
    diagonal = rows16 == cols16
    counted = jnp.where(diagonal & (rows16 < ROWS), 1.0, 0.0).astype(F32)

    zero = jnp.zeros((8, L_OWN), F32)
    sums = text_weights(0, (zero, zero))
    cosine = cosb[0:PAD, 0:128]
    logit = scale * cosine + shift
    other, same = sigmoid(logit), -sigmoid(-logit)
    wt[0:PAD, 0:128] = jnp.where(diagonal, same, other).astype(BF16)
    change = (same - other) * counted
    change_scale = change * cosine
    wait(*shared_l)
    sums = text_weights(1, sums)
    stat[0, 0:8, :] = (lanes(sums[0]) + change_scale[0:8] + change_scale[8:16]) * scale
    stat[0, 8:16, :] = lanes(sums[1]) + change[0:8] + change[8:16]

    def stat_send(level, devices):
        parts = [(stat.at[level], stat_in.at[level, i], d) for i, d in enumerate(devices)]
        return send_all(parts, stat_in.at[level, pl.ds(0, len(parts))])

    def stat_take(level, got, n):
        wait(got)
        total = stat[level]
        for i in range(n):
            total += stat_in[level, i]
        stat[level + 1] = total

    stat_got = stat_send(0, [at(dz=4), at(dz=-4)])
    wtc[...] = jnp.dot(sel[...], wt[...], preferred_element_type=F32).astype(BF16)

    def cols_of(k):
        return pl.ds(BEGINS[k], WIDTHS[k])

    x_in, z_in, x_out, z_out = {}, {}, {}, {}
    x_lo, x_hi = pl.ds(0, XR // 2), pl.ds(XR // 2, XR // 2)
    z_lo, z_hi = pl.ds(0, ZR // 2), pl.ds(ZR // 2, ZR // 2)

    def text_part(k):
        t = jnp.dot(wtc[:, 0:L_OWN], left[0][:, cols_of(k)], preferred_element_type=F32)
        t += jnp.dot(wtc[:, L_OWN : 2 * L_OWN], left[1][:, cols_of(k)], preferred_element_type=F32)
        tp[k][...] = t.reshape(NX, XR, WIDTHS[k])
        x_in[k] = [
            send(tp[k].at[2, x_lo], tx1[k].at[0], at(dx=1)),
            send(tp[k].at[2, x_hi], tx1[k].at[1], at(dx=-1)),
        ]

    def image_part(k):
        m = jnp.dot(wbc[:, 0:R_OWN], right[0][:, cols_of(k)], preferred_element_type=F32)
        m += jnp.dot(wbc[:, R_OWN : 2 * R_OWN], right[1][:, cols_of(k)], preferred_element_type=F32)
        ip[k][...] = m.reshape(NN, ZR, WIDTHS[k])
        z_in[k] = [
            send(ip[k].at[3, z_lo], iz1[k].at[0], at(dz=1)),
            send(ip[k].at[3, z_hi], iz1[k].at[1], at(dz=-1)),
        ]

    old = len(unsent)
    f_in, y_in = {}, {}

    def text_merge(k):
        wait(*x_in[k])
        tp[k][1, 0 : XR // 2] += tx1[k][0]
        tp[k][3, XR // 2 : XR] += tx1[k][1]
        x_out[k] = [send(tp[k].at[1], tx2[k].at[0], at(dx=1)), send(tp[k].at[3], tx2[k].at[1], at(dx=-1))]

    def image_merge(k):
        wait(*z_in[k])
        ip[k][1, 0 : ZR // 2] += iz1[k][0]
        ip[k][2, 0 : ZR // 2] += iz1[k][1]
        z_out[k] = [send(ip[k].at[1], iz2[k].at[0], at(dz=1)), send(ip[k].at[2], iz2[k].at[1], at(dz=-1))]

    for k in range(NC):
        text_part(k)
    image_weights(0)
    logit = scale * cosb[0:PAD, 0:128] + shift
    wb[0:PAD, 0:128] = jnp.where(diagonal, -sigmoid(-logit), sigmoid(logit)).astype(BF16)
    wait(*shared_r)
    image_weights(1)
    wbc[...] = jnp.dot(sel[0 : NN * ZR, 0:L_OWN], wb[...], preferred_element_type=F32).astype(BF16)
    image_part(0)
    text_merge(0)
    image_part(1)
    image_part(2)
    stat_take(0, stat_got, 2)
    stat_got = send(stat_in.at[0, 0], stat_in.at[1, 0], at(dz=4))
    image_merge(0)
    text_merge(1)
    image_merge(1)
    wait_sent(old)
    text_merge(2)
    image_merge(2)
    old = len(unsent)

    def image_far(k):
        over, other = (2, 3) if k % 2 == 0 else (3, 2)
        wait(*z_out[k])
        ip[k][0] += iz2[k][0] + iz2[k][1]
        for e in (1, 2, 3):
            pack(zb[k].at[e - 1], ip[k].at[0], ROWS * e)
        f_in[k] = [
            send(zb[k].at[0], iw[k].at[0], at(dz=Z_FAR[over])),
            send(zb[k].at[other - 1], iw[k].at[other - 1], at(dz=Z_FAR[other])),
        ]

    def image_over(k):
        over = 2 if k % 2 == 0 else 3
        wait(f_in[k][0])
        zb[k][over - 1] += iw[k][0]
        f_in[k][0] = send(zb[k].at[over - 1], iw[k].at[over - 1], at(dz=Z_FAR[over]))

    def text_far(k):
        wait(*x_out[k])
        tp[k][0] += tx2[k][0] + tx2[k][1]
        for j in range(1, NY):
            pack(yb[k].at[j - 1], tp[k].at[0], ROWS * j)
        y_in[k] = send_all(
            [(yb[k].at[j - 1], ty[k].at[j - 1], at(dy=Y_OFF[j])) for j in (7, 5, 6, 3, 4, 1, 2)], ty[k]
        )

    image_far(0)
    text_far(0)
    stat_take(1, stat_got, 1)
    stat_got = stat_send(2, [at(dy=d) for d in Y_OFF[1:]])
    image_far(1)
    image_far(2)
    text_far(1)
    image_over(0)
    image_over(1)
    stat_take(2, stat_got, NY - 1)
    stat_got = stat_send(3, [at(dx=d) for d in (1, 2, 3)])
    text_far(2)
    image_over(2)

    wait_sent(old)

    def total_of(i, own, got, entries):
        for k in range(NC):
            unpack(total.at[i], BEGINS[k], sum(got[k][e - 1] for e in entries))
        return total[i] + jnp.concatenate([own[k][0, 0:ROWS] for k in range(NC)], axis=1)

    def back(ref, total, out_ref):
        u, inverse = unit(ref)
        grad = scale * total
        out_ref[...] = (grad - u * jnp.sum(u * grad, axis=1, keepdims=True)) * inverse

    stat_take(3, stat_got, NX - 1)
    stat_got = stat_send(4, [at(dz=d) for d in (2, 1, -1)])
    for k in range(NC):
        wait(*f_in[k])
    image_sums = total_of(0, ip, iw, (2, 3))
    stat_take(4, stat_got, 3)
    stat_got = stat_send(5, [at(dc=1)])
    back(img_ref, image_sums, ig_ref)
    for k in range(NC):
        wait(y_in[k])
    back(txt_ref, total_of(1, tp, ty, range(1, NY)), tg_ref)
    stat_take(5, stat_got, 1)
    st_ref[0] = jnp.sum(stat[6, 0:8, :])
    st_ref[1] = jnp.sum(stat[6, 8:16, :])
    wait_sent(len(unsent))


def per_part(*dims):
    return tuple(pltpu.VMEM(dims + (w,), F32) for w in WIDTHS)


def packed(n):
    return tuple(pltpu.VMEM((n, 8, w + halves(w)[0]), F32) for w in WIDTHS)


def shards(images, texts, log_scale, bias):
    vmem, smem = pl.BlockSpec(memory_space=pltpu.VMEM), pl.BlockSpec(memory_space=pltpu.SMEM)
    hbm = pl.BlockSpec(memory_space=pltpu.HBM)
    return pl.pallas_call(
        kernel,
        out_shape=(
            jax.ShapeDtypeStruct((ROWS, D), F32),
            jax.ShapeDtypeStruct((ROWS, D), F32),
            jax.ShapeDtypeStruct((2,), F32),
        ),
        in_specs=[hbm, hbm, smem, smem],
        out_specs=(vmem, vmem, smem),
        scratch_shapes=[
            pltpu.VMEM((ROWS, D), BF16),
            pltpu.VMEM((ROWS, D), BF16),
            pltpu.VMEM((2, NN, NF, PAD, D), BF16),
            pltpu.VMEM((2, NX, NY, PAD, D), BF16),
            pltpu.VMEM((R_OWN, R_OWN), F32),
            pltpu.VMEM((R_OWN, 2 * L_OWN), BF16),
            pltpu.VMEM((L_OWN, 2 * R_OWN), BF16),
            pltpu.VMEM((NX * XR, 2 * L_OWN), BF16),
            pltpu.VMEM((NN * ZR, 2 * R_OWN), BF16),
            pltpu.VMEM((NX * XR, R_OWN), BF16),
            per_part(NX, XR),
            per_part(2, XR // 2),
            per_part(2, XR),
            packed(NY - 1),
            packed(NY - 1),
            per_part(NN, ZR),
            per_part(2, ZR // 2),
            per_part(2, ZR),
            packed(NF - 1),
            packed(NF - 1),
            pltpu.VMEM((2, ROWS, D), F32),
            pltpu.VMEM((7, 16, 128), F32),
            pltpu.VMEM((6, NY - 1, 16, 128), F32),
            pltpu.SemaphoreType.DMA((2,)),
            pltpu.SemaphoreType.DMA((N_COPIES,)),
            pltpu.SemaphoreType.DMA((N_COPIES,)),
        ],
        compiler_params=pltpu.CompilerParams(
            collective_id=0, has_side_effects=True, vmem_limit_bytes=48 * 1024 * 1024
        ),
        cost_estimate=pl.CostEstimate(flops=3 * 2 * 512 * 512 * D, bytes_accessed=1 << 20, transcendentals=1 << 20),
        name="pair_gradients",
    )(images, texts, log_scale, bias)


def solution(mesh):
    rows = P(("dp", "group"), None)
    return jax.shard_map(
        shards, mesh=mesh, in_specs=(rows, rows, P(), P()), out_specs=(rows, rows, P()), check_vma=False
    )
```
